128 devices in a mesh: utt: 4 (over x), tm: 4 (over y_hi, core), wshard: 8 (over y_lo, z).
Axes of the slice: x: 4, y: 4 (y_hi: 2, y_lo: 2; y = y_hi * 2 + y_lo), z: 4, core: 2. Of those that a mesh axis runs over, the one named last changes fastest.
Arguments:
- frames: bfloat16 [32, 2048, 1536], P(('utt', 'wshard'), 'tm'), may hold values from -6 to 6
- lengths: int32 [32], P(('utt', 'wshard')), may hold values from 512 to 2048, as said below
- cotangent: bfloat16 [32, 2048, 1536], P(('utt', 'wshard'), 'tm'), may hold values from -6 to 6
- norm_gain: float32 [1536], replicated, may hold values from 0.1 to 1.9
- w_in: bfloat16 [1536, 3072], P(('tm', 'wshard')), may hold values from -0.15625 to 0.15625
- kernel: float32 [31, 1536], replicated, may hold values from -1 to 1
- mid_gain: float32 [1536], replicated, may hold values from 0.1 to 1.9
- w_out: bfloat16 [1536, 1536], P(('tm', 'wshard')), may hold values from -0.15625 to 0.15625
Outputs:
- mixed: bfloat16 [32, 2048, 1536], P(('utt', 'wshard'), 'tm')
- grad_frames: bfloat16 [32, 2048, 1536], P(('utt', 'wshard'), 'tm')
- grad_in: float32 [1536, 3072], P(('tm', 'wshard'))
- grad_out: float32 [1536, 1536], P(('tm', 'wshard'))
- grad_kernel: float32 [31, 1536], replicated
- grad_norm_gain: float32 [1536], replicated
- grad_mid_gain: float32 [1536], replicated
The draws below stay inside these ranges and needn't reach their ends.
Inputs may be any that keep to these rules, and one draw needn't show every extreme that they name: `lengths`: frames at or after an utterance's length are padding.
All inputs are finite; a program needn't handle non-finite values.
Results may differ from the reference program's by a relative error of at most 0.029.
Values may be sent and summed in bfloat16 or wider, within the bound.
A program may use at most 128 MiB of HBM per device.

```python
import jax
import jax.numpy as jnp
from jax import lax

D = 1536
KERNEL = 31
F_DEV = 512
TIME = 2048
UTTS = 32
N_TM = 4


def draw_lengths(key, part):
    key = jax.random.fold_in(key, 7)
    first_key, second_key = jax.random.split(key)
    lowest = TIME // 4
    values = jax.random.randint(first_key, (UTTS,), lowest, TIME + 1)
    shuffled = jax.random.permutation(second_key, UTTS)
    values = values.at[shuffled[0]].set(TIME).at[shuffled[1]].set(lowest)
    return values.astype(jnp.int32)


def shard_levels(key, dims, cuts, low, top_value):
    loudness = 1.0
    for position, shards_of in cuts:
        draws = jax.random.uniform(jax.random.fold_in(jax.random.fold_in(key, 6), position), (shards_of,), jnp.float32, low / len(cuts), top_value / len(cuts))
        loudness = loudness * jnp.repeat(jnp.exp(draws), dims[position] // shards_of).reshape((-1,) + (1,) * (len(dims) - 1 - position))
    return loudness


def gaussian(key, shape, spread, most, pieces=(), held_as=jnp.bfloat16):
    gain = shard_levels(key, shape, pieces, -0.22, 0.18) if pieces else 1.0
    entries = jax.random.normal(key, shape, jnp.float32) * spread * gain
    return jnp.minimum(jnp.maximum(entries, -most), most).astype(held_as)


def setup_inputs(seed: int = 0) -> dict:
    key_of = jax.random.split(jax.random.key(seed), 9)
    return {
        "frames": gaussian(key_of[0], (UTTS, TIME, D), 1.0, 6.0, ((0, 32), (1, 4))),
        "lengths": draw_lengths(jax.random.fold_in(key_of[8], 71), 0),
        "cotangent": gaussian(key_of[2], (UTTS, TIME, D), 1.0, 6.0, ((0, 32), (1, 4))),
        "norm_gain": jnp.clip(1.0 + 0.18 * jax.random.normal(key_of[3], (D,), jnp.float32), 0.1, 1.9),
        "w_in": gaussian(key_of[4], (D, 2 * D), D ** -0.5, 0.15625, ((0, 32),)),
        "kernel": gaussian(key_of[5], (KERNEL, D), KERNEL ** -0.5, 1.0, (), jnp.float32),
        "mid_gain": jnp.clip(1.0 + 0.18 * jax.random.normal(key_of[6], (D,), jnp.float32), 0.1, 1.9),
        "w_out": gaussian(key_of[7], (D, D), D ** -0.5, 0.15625, ((0, 32),)),
    }


EPS = 1e-05

def normalize(values):
    center = values - lax.optimization_barrier(jnp.mean(values, -1, keepdims=True))
    inverse = lax.rsqrt(lax.optimization_barrier(jnp.mean(center * center, -1, keepdims=True)) + EPS)
    return (center * inverse, inverse)

def norm_backward(upstream, normed, inverse):
    return inverse * (upstream - lax.optimization_barrier(jnp.mean(upstream, -1, keepdims=True)) - normed * lax.optimization_barrier(jnp.mean(upstream * normed, -1, keepdims=True)))

def block_partials(left, right):
    left_blocks = left.astype(jnp.float32).reshape(N_TM, F_DEV, -1)
    right_blocks = right.astype(jnp.float32).reshape(N_TM, F_DEV, -1)
    partial_sums = jnp.einsum('tfd,tfe->tde', left_blocks, right_blocks)
    rounded = lax.optimization_barrier(partial_sums.astype(jnp.bfloat16))
    return lax.optimization_barrier(jnp.sum(rounded.astype(jnp.float32), 0))

def utterance(frames_one, length_one, upstream_one, norm_gain, w_in, kernel, mid_gain, w_out):
    reach = KERNEL // 2
    valid = (jnp.arange(TIME, dtype=jnp.int32) < length_one).astype(jnp.float32)[:, None]
    inputs = frames_one.astype(jnp.float32)
    centred, inverse_in = normalize(inputs)
    normed = (centred * norm_gain).astype(jnp.bfloat16)
    hidden = jnp.dot(normed, w_in, preferred_element_type=jnp.float32)
    linear = hidden[:, :D]
    opened = jax.nn.sigmoid(hidden[:, D:])
    gated = (linear * opened * valid).astype(jnp.bfloat16)
    padded = jnp.pad(gated.astype(jnp.float32), ((reach, reach), (0, 0)))
    temporal = jnp.zeros((TIME, D), jnp.float32)
    for offset in range(KERNEL):
        temporal = temporal + kernel[offset] * padded[offset:offset + TIME]
    mid_hat, inverse_mid = normalize(temporal)
    mid_normed = mid_hat * mid_gain
    mid_sigmoid = jax.nn.sigmoid(mid_normed)
    smooth = (mid_normed * mid_sigmoid).astype(jnp.bfloat16)
    branch = jnp.dot(smooth, w_out, preferred_element_type=jnp.float32)
    mixed = (inputs + valid * branch).astype(jnp.bfloat16)
    branch_grad = (upstream_one.astype(jnp.float32) * valid).astype(jnp.bfloat16)
    smooth_grad = jnp.dot(branch_grad, w_out.T, preferred_element_type=jnp.float32)
    mid_grad = smooth_grad * (mid_sigmoid * (1.0 + mid_normed * (1.0 - mid_sigmoid)))
    mid_term = lax.optimization_barrier(jnp.sum(mid_grad * mid_hat, 0))
    temporal_grad = norm_backward(mid_grad * mid_gain, mid_hat, inverse_mid).astype(jnp.bfloat16)
    temporal_full = temporal_grad.astype(jnp.float32)
    grad_padded = jnp.pad(temporal_full, ((reach, reach), (0, 0)))
    gated_grad = jnp.zeros((TIME, D), jnp.float32)
    kernel_rows = []
    for offset in range(KERNEL):
        gated_grad = gated_grad + kernel[offset] * grad_padded[2 * reach - offset:2 * reach - offset + TIME]
        kernel_rows.append(lax.optimization_barrier(jnp.sum(padded[offset:offset + TIME] * temporal_full, 0)))
    kernel_term = jnp.stack(kernel_rows)
    gated_grad = gated_grad * valid
    hidden_grad = jnp.concatenate([gated_grad * opened, gated_grad * linear * opened * (1.0 - opened)], 1).astype(jnp.bfloat16)
    normed_grad = jnp.dot(hidden_grad, w_in.T, preferred_element_type=jnp.float32)
    in_term = lax.optimization_barrier(jnp.sum(normed_grad * centred, 0))
    grad_frames = (upstream_one.astype(jnp.float32) + norm_backward(normed_grad * norm_gain, centred, inverse_in)).astype(jnp.bfloat16)
    in_part = block_partials(normed, hidden_grad)
    out_part = block_partials(smooth, branch_grad)
    return (mixed, grad_frames, in_part, out_part, kernel_term, in_term, mid_term)

def reference(frames, lengths, cotangent, norm_gain, w_in, kernel, mid_gain, w_out):

    def scan_step(carry, packed):
        frames_one, length_one, upstream_one = packed
        mixed, grad_frames, in_part, out_part, kernel_term, in_term, mid_term = utterance(frames_one, length_one, upstream_one, norm_gain, w_in, kernel, mid_gain, w_out)
        totals = (carry[0] + in_part, carry[1] + out_part, carry[2] + kernel_term, carry[3] + in_term, carry[4] + mid_term)
        return (totals, (mixed, grad_frames))
    start = (jnp.zeros((D, 2 * D), jnp.float32), jnp.zeros((D, D), jnp.float32), jnp.zeros((KERNEL, D), jnp.float32), jnp.zeros((D,), jnp.float32), jnp.zeros((D,), jnp.float32))
    totals, stacked = lax.scan(scan_step, start, (frames, lengths, cotangent))
    norm_scale = float(UTTS * TIME) ** (-0.5)
    return (stacked[0], stacked[1], totals[0] * norm_scale, totals[1] * norm_scale, totals[2] * norm_scale, totals[3] * norm_scale, totals[4] * norm_scale)
```

```python
import functools
import math

import jax
import jax.numpy as jnp
from jax import lax
from jax.experimental import pallas as pl
from jax.experimental.pallas import tpu as pltpu
from jax.sharding import PartitionSpec as P

EPS = 1e-05
MESH = pl.DeviceIdType.MESH
F32 = jnp.float32
BF16 = jnp.bfloat16
ROWS = 48


def around(value, shift):
    return lax.rem(value + shift, 4)


class Place:
    def __init__(self):
        tm, ws = lax.axis_index("tm"), lax.axis_index("wshard")
        self.x = lax.axis_index("utt")
        self.c = lax.rem(tm, 2)
        self.y = lax.div(tm, 2) * 2 + lax.div(ws, 4)
        self.z = lax.rem(ws, 4)

    def device(self, x, y, z, c):
        return (x, lax.div(y, 2) * 2 + c, lax.rem(y, 2) * 4 + z)

    def at(self, axis, shift):
        x, y, z = self.x, self.y, self.z
        if axis == "x":
            x = around(x, shift)
        if axis == "y":
            y = around(y, shift)
        if axis == "z":
            z = around(z, shift)
        return self.device(x, y, z, self.c)

    def sibling(self):
        return self.device(self.x, self.y, self.z, 1 - self.c)

    def greet(self):
        barrier = pltpu.get_barrier_semaphore()
        others = [self.at(axis, shift) for axis in "xyz" for shift in (1, 2, 3)]
        others.append(self.sibling())
        for other in others:
            pl.semaphore_signal(barrier, inc=1, device_id=other, device_id_type=MESH)
        pl.semaphore_wait(barrier, len(others))


class Net:
    def __init__(self, place, sent, landed):
        self.place, self.sent, self.landed = place, sent, landed
        self.count = 0
        self.flying = []

    def send(self, src, dst, device):
        slot = self.count
        self.count += 1
        copy = pltpu.make_async_remote_copy(
            src_ref=src,
            dst_ref=dst,
            send_sem=self.sent.at[slot],
            recv_sem=self.landed.at[slot],
            device_id=device,
            device_id_type=MESH,
        )
        copy.start()
        self.flying.append(copy)
        return slot

    def wait(self, slot, dst):
        pltpu.make_async_remote_copy(
            src_ref=dst,
            dst_ref=dst,
            send_sem=self.sent.at[slot],
            recv_sem=self.landed.at[slot],
            device_id=self.place.sibling(),
            device_id_type=MESH,
        ).wait_recv()

    def drain(self):
        for copy in self.flying:
            copy.wait_send()
        self.flying = []


class Gather:
    def __init__(self, net, place, full):
        self.net, self.place, self.full = net, place, full
        self.portion = full.shape[-1] // 3
        self.quarter = self.portion // 4

    def part_a(self, dy, dz):
        p = self.place
        y = around(p.y, 4 - dy)
        z = around(p.z, 4 - dz)
        return self.full.at[p.c, y, z, :, pl.ds(0, self.portion)]

    def part_b(self, dy, dz):
        p = self.place
        y = around(p.y, 4 - dy)
        z = around(p.z, 4 - dz)
        return self.full.at[p.c, y, z, :, pl.ds(self.portion, self.portion)]

    def columns(self, which, dx):
        x = around(self.place.x, 4 - dx)
        start = pl.multiple_of(which * self.portion + x * self.quarter, 128)
        return pl.ds(start, self.quarter)

    def quarter_b(self, dy, dx):
        p = self.place
        return self.full.at[p.c, around(p.y, 4 - dy), p.z, :, self.columns(1, dx)]

    def quarter_c(self, dy, dz, dx):
        p = self.place
        return self.full.at[
            p.c, around(p.y, 4 - dy), around(p.z, 4 - dz), :, self.columns(2, dx)
        ]

    def group_c(self, group, dx):
        p = self.place
        dy, dz = group
        if dz is None:
            return self.full.at[p.c, around(p.y, 4 - dy), :, :, self.columns(2, dx)]
        return self.quarter_c(dy, dz, dx)

    def share(self, name, c):
        p = self.place
        kind, shift = name
        if kind == "a":
            return self.full.at[c, around(p.y, 4 - shift), :, :, pl.ds(0, self.portion)]
        if kind == "b":
            return self.full.at[
                c, :, around(p.z, 4 - shift), :, pl.ds(self.portion, self.portion)
            ]
        return self.full.at[c, :, :, :, self.columns(2, shift)]

    def give(self, name):
        ref = self.share(name, self.place.c)
        self.shared.append((name, self.net.send(ref, ref, self.place.sibling())))

    def begin(self):
        net, p = self.net, self.place
        self.shared = []
        own_b, own_c = self.quarter_b(0, 0), self.quarter_c(0, 0, 0)
        own_a, own_whole_b = self.part_a(0, 0), self.part_b(0, 0)
        self.c_z, self.b_y, self.a_z = {}, {}, {}
        self.c_y, self.a_y, self.b_z = {}, {}, {}
        self.c_x, self.b_x = {}, {}
        for shift in (1, 3, 2):
            self.c_z[shift] = net.send(own_c, own_c, p.at("z", shift))
            self.b_y[shift] = net.send(own_b, own_b, p.at("y", shift))
        for shift in (1, 3, 2):
            self.a_z[shift] = net.send(own_a, own_a, p.at("z", shift))
            self.c_y[shift, 0] = net.send(own_c, own_c, p.at("y", shift))
        for shift in (1, 3):
            self.a_y[shift, 0] = net.send(own_a, own_a, p.at("y", shift))
            self.b_z[shift, 0] = net.send(own_whole_b, own_whole_b, p.at("z", shift))

    def second(self):
        net, p = self.net, self.place
        for d in (1, 3, 2):
            ref = self.quarter_c(0, d, 0)
            net.wait(self.c_z[d], ref)
            for shift in (1, 3, 2):
                self.c_y[shift, d] = net.send(ref, ref, p.at("y", shift))
            for shift in (1, 3):
                self.c_x[shift, (0, d)] = net.send(ref, ref, p.at("x", shift))
            ref = self.quarter_b(d, 0)
            net.wait(self.b_y[d], ref)
            for shift in (1, 3, 2):
                self.b_x[shift, d] = net.send(ref, ref, p.at("x", shift))
        for d in (1, 3, 2):
            ref = self.part_a(0, d)
            net.wait(self.a_z[d], ref)
            for shift in (1, 3):
                self.a_y[shift, d] = net.send(ref, ref, p.at("y", shift))
        self.give(("a", 0))

    def third(self):
        net, p = self.net, self.place
        for d in (1, 3, 2):
            for shift in (1, 3, 2):
                net.wait(self.b_x[shift, d], self.quarter_b(d, shift))
            ref = self.part_b(d, 0)
            for shift in (1, 3):
                self.b_z[shift, d] = net.send(ref, ref, p.at("z", shift))
            for dz in range(4):
                net.wait(self.c_y[d, dz], self.quarter_c(d, dz, 0))
            ref = self.group_c((d, None), 0)
            for shift in (1, 3):
                self.c_x[shift, (d, None)] = net.send(ref, ref, p.at("x", shift))
        self.give(("b", 0))
        self.give(("c", 0))

    def onward(self, table, keys, region, axis):
        net, p = self.net, self.place
        far = {}
        for number, key in enumerate(keys):
            for shift in (1, 3):
                ref = region(key, shift)
                net.wait(table[shift, key], ref)
                if (number % 2 == 0) == (shift == 1):
                    far[key] = net.send(ref, ref, p.at(axis, shift))
        return far

    def fourth(self):
        groups = [(0, 1), (0, 3), (0, 2), (1, None), (3, None), (2, None)]
        self.groups = groups
        self.a_far = self.onward(self.a_y, (0, 1, 3, 2), lambda d, s: self.part_a(s, d), "y")
        self.b_far = self.onward(self.b_z, (0, 1, 3, 2), lambda d, s: self.part_b(d, s), "z")
        self.c_far = self.onward(self.c_x, groups, lambda g, s: self.group_c(g, s), "x")
        for shift in (1, 3):
            for kind in "abc":
                self.give((kind, shift))

    def finish(self):
        net, p = self.net, self.place
        for d in (0, 1, 3, 2):
            net.wait(self.a_far[d], self.part_a(2, d))
        self.give(("a", 2))
        for d in (0, 1, 3, 2):
            net.wait(self.b_far[d], self.part_b(d, 2))
        self.give(("b", 2))
        for group in self.groups:
            net.wait(self.c_far[group], self.group_c(group, 2))
        self.give(("c", 2))
        for name, slot in self.shared:
            net.wait(slot, self.share(name, 1 - p.c))


GATHER_COPIES = 90


def add_into(target, term):
    target[...] = (target[...].astype(F32) + term[...].astype(F32)).astype(target.dtype)


class Scatter:
    def __init__(self, net, place, terms, spare, bufs):
        self.net, self.place, self.terms, self.spare = net, place, terms, spare
        self.portion = terms.shape[-1] // 3
        self.quarter = self.portion // 4
        self.near, self.mid, self.final, self.done = bufs
        self.slots = {}

    @staticmethod
    def scratch(columns):
        portion, quarter = columns // 3, columns // 12
        return [
            [
                pltpu.VMEM((2, 2, ROWS, portion), BF16),
                pltpu.VMEM((2, 2, ROWS, portion), BF16),
                pltpu.VMEM((2, 2, 4, ROWS, quarter), BF16),
                pltpu.VMEM((2, 4, ROWS, portion), BF16),
                pltpu.VMEM((2, 4, ROWS, portion), BF16),
                pltpu.VMEM((2, 4, 4, ROWS, quarter), BF16),
            ],
            [
                pltpu.VMEM((3, ROWS, portion), BF16),
                pltpu.VMEM((3, 4, ROWS, quarter), BF16),
                pltpu.VMEM((3, 4, ROWS, quarter), BF16),
            ],
            [pltpu.VMEM((3, ROWS, quarter), BF16)] * 3,
            pltpu.VMEM((4, 3, ROWS, quarter), BF16),
        ]

    def columns(self, which, x):
        start = pl.multiple_of(which * self.portion + x * self.quarter, 128)
        return pl.ds(start, self.quarter)

    def whole(self, which):
        return pl.ds(which * self.portion, self.portion)

    def first(self, which, shift, of, half=None):
        p = self.place
        part = slice(None) if half is None else pl.ds(2 * half, 2)
        if which == 0:
            return of.at[around(p.y, shift), part, :, self.whole(0)]
        if which == 1:
            return of.at[part, around(p.z, shift), :, self.whole(1)]
        return of.at[part, :, :, self.columns(2, around(p.x, shift))]

    def second(self, which, shift):
        p, mine = self.place, self.mine()
        if which == 0:
            return mine.at[p.y, around(p.z, shift), :, self.whole(0)]
        if which == 1:
            return mine.at[:, p.z, :, self.columns(1, around(p.x, shift))]
        return mine.at[around(p.y, shift), :, :, self.columns(2, p.x)]

    def third(self, which, shift):
        p, mine = self.place, self.mine()
        if which == 0:
            return mine.at[p.y, p.z, :, self.columns(0, around(p.x, shift))]
        if which == 1:
            return mine.at[around(p.y, shift), p.z, :, self.columns(1, p.x)]
        return mine.at[p.y, around(p.z, shift), :, self.columns(2, p.x)]

    def mine(self):
        return self.terms.at[self.place.c]

    AXES = (("y", "z", "x"), ("z", "x", "y"), ("x", "y", "z"))

    def to_sibling(self):
        p = self.place
        for shift in (2, 1, 3, 0):
            for which in range(3):
                self.slots["pair", which, shift] = self.net.send(
                    self.first(which, shift, self.terms.at[1 - p.c]),
                    self.first(which, shift, self.spare),
                    p.sibling(),
                )

    def pair(self, which, shift):
        term = self.first(which, shift, self.spare)
        self.net.wait(self.slots["pair", which, shift], term)
        target = self.first(which, shift, self.mine())
        for i in range(4):
            add_into(target.at[i], term.at[i])

    def step_far(self):
        net, p = self.net, self.place
        for which in range(3):
            axis = self.AXES[which][0]
            self.pair(which, 2)
            for half, shift in ((0, 1), (1, 3)):
                self.slots["far", which, half] = net.send(
                    self.first(which, 2, self.mine(), half),
                    self.near[which].at[half],
                    p.at(axis, shift),
                )

    def step_near(self):
        net, p = self.net, self.place
        for which in range(3):
            axis = self.AXES[which][0]
            self.pair(which, 1)
            self.pair(which, 3)
            for half, shift in ((0, 1), (1, 3)):
                came = self.near[which].at[half]
                net.wait(self.slots["far", which, half], came)
                target = self.first(which, shift, self.mine(), half)
                for i in range(2):
                    add_into(target.at[i], came.at[i])
                self.slots["near", which, half] = net.send(
                    self.first(which, shift, self.mine()),
                    self.near[3 + which].at[half],
                    p.at(axis, shift),
                )

    def step_second(self):
        net, p = self.net, self.place
        for which in range(3):
            axis = self.AXES[which][1]
            self.pair(which, 0)
            target = self.first(which, 0, self.mine())
            for half in range(2):
                came = self.near[3 + which].at[half]
                net.wait(self.slots["near", which, half], came)
                for i in range(4):
                    add_into(target.at[i], came.at[i])
            for shift in (2, 1, 3):
                self.slots["second", which, shift] = net.send(
                    self.second(which, shift), self.mid[which].at[shift - 1], p.at(axis, shift)
                )

    def step_third(self):
        net, p = self.net, self.place
        for which in range(3):
            axis = self.AXES[which][2]
            target = self.second(which, 0)
            for shift in (1, 3, 2):
                came = self.mid[which].at[shift - 1]
                net.wait(self.slots["second", which, shift], came)
                if which == 0:
                    add_into(target, came)
                else:
                    for i in range(4):
                        add_into(target.at[i], came.at[i])
            for shift in (2, 1, 3):
                self.slots["third", which, shift] = net.send(
                    self.third(which, shift), self.final[which].at[shift - 1], p.at(axis, shift)
                )

    def step_spread(self):
        net, p = self.net, self.place
        for which in range(3):
            total = self.third(which, 0)[...].astype(F32)
            for shift in (1, 3, 2):
                came = self.final[which].at[shift - 1]
                net.wait(self.slots["third", which, shift], came)
                total = total + came[...].astype(F32)
            self.done[p.x, which] = total.astype(BF16)
        for shift in (2, 1, 3):
            self.slots["spread", shift] = net.send(
                self.done.at[p.x], self.done.at[p.x], p.at("x", shift)
            )

    def step_last(self, out, scale):
        net, p = self.net, self.place
        for shift in (1, 3, 2):
            net.wait(self.slots["spread", shift], self.done.at[around(p.x, 4 - shift)])
        for which in range(3):
            for x in range(4):
                start = which * self.portion + x * self.quarter
                out[:, start : start + self.quarter] = self.done[x, which].astype(F32) * scale


SCATTER_COPIES = 48


class Total:
    ORDERS = ("xyz", "yzx", "zxy")

    def __init__(self, net, place, terms, pair, stages, out):
        self.net, self.place, self.terms, self.pairbuf = net, place, terms, pair
        self.stages, self.out = stages, out
        self.slots = {}

    @staticmethod
    def scratch(rows, width):
        return [
            pltpu.VMEM((3, rows, width), F32),
            pltpu.VMEM((3, 3, 4, rows, width), F32),
        ]

    def coordinate(self, axis):
        return {"x": self.place.x, "y": self.place.y, "z": self.place.z}[axis]

    def to_sibling(self):
        p = self.place
        self.slots["pair"] = self.net.send(self.terms.at[1 - p.c], self.pairbuf, p.sibling())

    def put(self, stage, portion, value):
        axis = self.ORDERS[portion][stage]
        own = self.stages.at[stage, portion, self.coordinate(axis)]
        own[...] = value
        for shift in (2, 1, 3):
            self.slots[stage, portion, shift] = self.net.send(own, own, self.place.at(axis, shift))

    def begin(self):
        self.net.wait(self.slots["pair"], self.pairbuf)
        for portion in range(3):
            self.put(0, portion, self.terms[self.place.c, portion] + self.pairbuf[portion])

    def collect(self, stage, portion):
        axis = self.ORDERS[portion][stage]
        for shift in (1, 3, 2):
            other = around(self.coordinate(axis), 4 - shift)
            self.net.wait(self.slots[stage, portion, shift], self.stages.at[stage, portion, other])
        s = self.stages
        return (s[stage, portion, 0] + s[stage, portion, 1]) + (
            s[stage, portion, 2] + s[stage, portion, 3]
        )

    def step(self, stage):
        for portion in range(3):
            self.put(stage, portion, self.collect(stage - 1, portion))

    def spread(self):
        p = self.place
        for portion in range(3):
            self.out[p.c, portion] = self.collect(2, portion)
        self.slots["back"] = self.net.send(self.out.at[p.c], self.out.at[p.c], p.sibling())

    def last(self):
        self.net.wait(self.slots["back"], self.out.at[1 - self.place.c])


TOTAL_COPIES = 32


def gather_kernel(in_ref, out_ref, in_full, out_full, sent, landed, local):
    place = Place()
    net = Net(place, sent, landed)
    loads = []
    for i, (shard, full) in enumerate(((in_ref, in_full), (out_ref, out_full))):
        copy = pltpu.make_async_copy(shard, full.at[place.c, place.y, place.z], local.at[i])
        copy.start()
        loads.append(copy)
    place.greet()
    loads[0].wait()
    loads[1].wait()
    first = Gather(net, place, in_full)
    second = Gather(net, place, out_full)
    first.begin()
    first.second()
    second.begin()
    first.third()
    second.second()
    first.fourth()
    second.third()
    first.finish()
    second.fourth()
    second.finish()
    net.drain()


def gather_all(w_in, w_out):
    anywhere = pl.BlockSpec(memory_space=pl.ANY)
    return pl.pallas_call(
        gather_kernel,
        out_shape=[
            jax.ShapeDtypeStruct((2, 4, 4, ROWS, w.shape[1]), BF16) for w in (w_in, w_out)
        ],
        in_specs=[anywhere] * 2,
        out_specs=[anywhere] * 2,
        scratch_shapes=[
            pltpu.SemaphoreType.DMA((2 * GATHER_COPIES,)),
            pltpu.SemaphoreType.DMA((2 * GATHER_COPIES,)),
            pltpu.SemaphoreType.DMA((2,)),
        ],
        compiler_params=pltpu.CompilerParams(collective_id=0, has_side_effects=True),
    )(w_in, w_out)


def flatten(tree):
    return jax.tree_util.tree_flatten(tree)


def scatter_kernel(scale, jobs, tree, *refs):
    inputs, refs = refs[: jobs + 1], refs[jobs + 1 :]
    outs, refs = refs[: jobs + 1], refs[jobs + 1 :]
    terms, refs = refs[:jobs], refs[jobs:]
    spares, refs = refs[:jobs], refs[jobs:]
    small, sent, landed, local = refs[:4]
    bufs = jax.tree_util.tree_unflatten(tree, refs[4:])
    place = Place()
    net = Net(place, sent, landed)
    loads = []
    for i, (src, dst) in enumerate(zip(inputs, list(terms) + [small])):
        copy = pltpu.make_async_copy(src, dst, local.at[i])
        copy.start()
        loads.append(copy)
    place.greet()
    scatters = [Scatter(net, place, t, s, b) for t, s, b in zip(terms, spares, bufs[:jobs])]
    total = Total(net, place, small, *bufs[jobs], outs[jobs])
    for copy in loads:
        copy.wait()
    for s in scatters:
        s.to_sibling()
    total.to_sibling()
    for s in scatters:
        s.step_far()
    total.begin()
    for s in scatters:
        s.step_near()
    total.step(1)
    for s in scatters:
        s.step_second()
    total.step(2)
    for s in scatters:
        s.step_third()
    total.spread()
    for s in scatters:
        s.step_spread()
    for s, out in zip(scatters, outs):
        s.step_last(out, scale)
    total.last()
    net.drain()


def scatter_all(partials, small, scale):
    jobs = len(partials)
    columns = partials[0].shape[-1]
    bufs = [Scatter.scratch(columns) for _ in partials]
    bufs.append(Total.scratch(*small.shape[2:]))
    leaves, tree = flatten(bufs)
    anywhere = pl.BlockSpec(memory_space=pl.ANY)
    inside = pl.BlockSpec(memory_space=pltpu.VMEM)
    copies = jobs * SCATTER_COPIES + TOTAL_COPIES
    return pl.pallas_call(
        functools.partial(scatter_kernel, scale, jobs, tree),
        out_shape=[jax.ShapeDtypeStruct((ROWS, columns), F32) for _ in partials]
        + [jax.ShapeDtypeStruct(small.shape, F32)],
        in_specs=[anywhere] * (jobs + 1),
        out_specs=[inside] * (jobs + 1),
        scratch_shapes=[pltpu.VMEM(t.shape, BF16) for t in partials]
        + [pltpu.VMEM(t.shape[1:], BF16) for t in partials]
        + [
            pltpu.VMEM(small.shape, F32),
            pltpu.SemaphoreType.DMA((copies,)),
            pltpu.SemaphoreType.DMA((copies,)),
            pltpu.SemaphoreType.DMA((jobs + 1,)),
        ]
        + leaves,
        compiler_params=pltpu.CompilerParams(
            collective_id=1, has_side_effects=True, vmem_limit_bytes=60 * 2**20
        ),
    )(*partials, small)


def by_owner(partial):
    columns = partial.shape[1]
    return (
        partial.reshape(2, 2, 8 * ROWS, columns).swapaxes(0, 1).reshape(2, 4, 4, ROWS, columns)
    )


def in_order(full):
    columns = full.shape[-1]
    return full.reshape(2, 2, 8 * ROWS, columns).swapaxes(0, 1).reshape(-1, columns)


def extended(array, sides, width):
    for axis, dim in sides:
        devices, length = (lax.axis_size(axis), array.shape[dim])
        up = [(i, (i + 1) % devices) for i in range(devices - 1)]
        down = [(j, i) for i, j in up]
        last = lax.slice_in_dim(array, length - width, length, axis=dim)
        first = lax.slice_in_dim(array, 0, width, axis=dim)
        before = lax.ppermute(last, axis, up)
        after = lax.ppermute(first, axis, down)
        array = jnp.concatenate([before, array, after], axis=dim)
    return array


def normalize(values):
    center = values - jnp.mean(values, -1, keepdims=True)
    inverse = lax.rsqrt(jnp.mean(center * center, -1, keepdims=True) + EPS)
    return (center * inverse, inverse)


def norm_backward(upstream, normed, inverse):
    return inverse * (
        upstream
        - jnp.mean(upstream, -1, keepdims=True)
        - normed * jnp.mean(upstream * normed, -1, keepdims=True)
    )


def product_last(left, right):
    return lax.dot_general(
        left, right, (((1,), (1,)), ((), ())), preferred_element_type=jnp.float32
    )


def product_first(left, right):
    return lax.dot_general(
        left, right, (((0,), (0,)), ((), ())), preferred_element_type=jnp.float32
    )


def body(frames, lengths, cotangent, norm_gain, w_in, kernel, mid_gain, w_out):
    utterances, seq_rows, feature_dim = frames.shape
    kernel_len = kernel.shape[0]
    reach = kernel_len // 2
    norm_scale = 1.0 / math.sqrt(
        utterances * seq_rows * lax.axis_size("utt") * lax.axis_size("tm") * lax.axis_size("wshard")
    )
    positions = lax.axis_index("tm") * seq_rows + lax.iota(jnp.int32, seq_rows)
    valid = (positions[None, :] < lengths[:, None]).astype(jnp.float32).reshape(-1, 1)
    inputs = frames.reshape(-1, feature_dim).astype(jnp.float32)
    upstream = cotangent.reshape(-1, feature_dim).astype(jnp.float32)
    in_full, out_full = gather_all(w_in, w_out)
    in_full, out_full = in_order(in_full), in_order(out_full)
    centred, inverse_in = normalize(inputs)
    normed = (centred * norm_gain).astype(jnp.bfloat16)
    hidden = jnp.dot(normed, in_full, preferred_element_type=jnp.float32)
    linear = hidden[:, :feature_dim]
    opened = jax.nn.sigmoid(hidden[:, feature_dim:])
    gated = (linear * opened * valid).astype(jnp.bfloat16)
    padded = extended(gated.reshape(utterances, seq_rows, feature_dim), (("tm", 1),), reach).astype(
        jnp.float32
    )
    temporal = jnp.zeros((utterances, seq_rows, feature_dim), jnp.float32)
    for offset in range(kernel_len):
        temporal = temporal + kernel[offset] * padded[:, offset : offset + seq_rows]
    mid_hat, inverse_mid = normalize(temporal.reshape(-1, feature_dim))
    mid_normed = mid_hat * mid_gain
    mid_sigmoid = jax.nn.sigmoid(mid_normed)
    smooth = (mid_normed * mid_sigmoid).astype(jnp.bfloat16)
    branch = jnp.dot(
        smooth,
        out_full,
        preferred_element_type=jnp.float32,
    )
    mixed = (
        (inputs + valid * branch).astype(jnp.bfloat16).reshape(utterances, seq_rows, feature_dim)
    )
    branch_grad = (upstream * valid).astype(jnp.bfloat16)
    smooth_grad = product_last(
        branch_grad, out_full
    )
    mid_grad = smooth_grad * (mid_sigmoid * (1.0 + mid_normed * (1.0 - mid_sigmoid)))
    mid_term = jnp.sum(mid_grad * mid_hat, 0)
    temporal_grad = norm_backward(mid_grad * mid_gain, mid_hat, inverse_mid).astype(jnp.bfloat16)
    temporal_grad = temporal_grad.reshape(utterances, seq_rows, feature_dim)
    grad_padded = extended(temporal_grad, (("tm", 1),), reach).astype(jnp.float32)
    temporal_full = temporal_grad.astype(jnp.float32)
    gated_grad = jnp.zeros((utterances, seq_rows, feature_dim), jnp.float32)
    kernel_rows = []
    for offset in range(kernel_len):
        gated_grad = (
            gated_grad
            + kernel[offset] * grad_padded[:, 2 * reach - offset : 2 * reach - offset + seq_rows]
        )
        kernel_rows.append(jnp.sum(padded[:, offset : offset + seq_rows] * temporal_full, (0, 1)))
    kernel_term = jnp.stack(kernel_rows)
    gated_grad = gated_grad.reshape(-1, feature_dim) * valid
    hidden_grad = jnp.concatenate(
        [gated_grad * opened, gated_grad * linear * opened * (1.0 - opened)], 1
    ).astype(jnp.bfloat16)
    normed_grad = product_last(hidden_grad, in_full)
    in_term = jnp.sum(normed_grad * centred, 0)
    grad_frames = (upstream + norm_backward(normed_grad * norm_gain, centred, inverse_in)).astype(
        jnp.bfloat16
    )
    grad_frames = grad_frames.reshape(utterances, seq_rows, feature_dim)
    in_part = product_first(normed, hidden_grad).astype(BF16)
    out_part = product_first(smooth, branch_grad).astype(BF16)
    half = feature_dim // 2
    parts = [out_part] + [
        jnp.concatenate(
            [in_part[:, s : s + half], in_part[:, feature_dim + s : feature_dim + s + half]], 1
        )
        for s in (0, half)
    ]
    small = jnp.concatenate(
        [kernel_term, in_term[None], mid_term[None], jnp.zeros((7, feature_dim), F32)]
    )
    small = small.reshape(40, 3, 2, 256).transpose(2, 1, 0, 3)
    grad_out, first, second, small = scatter_all([by_owner(p) for p in parts], small, norm_scale)
    grad_in = jnp.concatenate(
        [first[:, :half], second[:, :half], first[:, half:], second[:, half:]], 1
    )
    small = small.transpose(2, 1, 0, 3).reshape(40, feature_dim)
    kernel_sum, in_gain_sum, mid_gain_sum = small[:kernel_len], small[kernel_len], small[kernel_len + 1]
    return (
        mixed,
        grad_frames,
        grad_in,
        grad_out,
        kernel_sum * norm_scale,
        in_gain_sum * norm_scale,
        mid_gain_sum * norm_scale,
    )


def solution(mesh):
    return jax.shard_map(
        body,
        mesh=mesh,
        in_specs=(
            P(("utt", "wshard"), "tm", None),
            P(("utt", "wshard")),
            P(("utt", "wshard"), "tm", None),
            P(),
            P(("tm", "wshard"), None),
            P(),
            P(),
            P(("tm", "wshard"), None),
        ),
        out_specs=(
            P(("utt", "wshard"), "tm", None),
            P(("utt", "wshard"), "tm", None),
            P(("tm", "wshard"), None),
            P(("tm", "wshard"), None),
            P(),
            P(),
            P(),
        ),
        check_vma=False,
    )
```

```python
import functools
import math

import jax
import jax.numpy as jnp
from jax import lax
from jax.experimental import pallas as pl
from jax.experimental.pallas import tpu as pltpu
from jax.sharding import PartitionSpec as P

EPS = 1e-05
MESH = pl.DeviceIdType.MESH
F32 = jnp.float32
BF16 = jnp.bfloat16
ROWS = 48
D = 1536
FRAMES = 512
HALF = D // 2


def around(value, shift):
    return lax.rem(value + shift, 4)


class Place:
    def __init__(self):
        tm, ws = lax.axis_index("tm"), lax.axis_index("wshard")
        self.x = lax.axis_index("utt")
        self.c = lax.rem(tm, 2)
        self.y = lax.div(tm, 2) * 2 + lax.div(ws, 4)
        self.z = lax.rem(ws, 4)

    def device(self, x, y, z, c):
        return (x, lax.div(y, 2) * 2 + c, lax.rem(y, 2) * 4 + z)

    def at(self, axis, shift):
        x, y, z = self.x, self.y, self.z
        if axis == "x":
            x = around(x, shift)
        if axis == "y":
            y = around(y, shift)
        if axis == "z":
            z = around(z, shift)
        return self.device(x, y, z, self.c)

    def sibling(self):
        return self.device(self.x, self.y, self.z, 1 - self.c)

    def greet(self):
        barrier = pltpu.get_barrier_semaphore()
        others = [self.at(axis, shift) for axis in "xyz" for shift in (1, 2, 3)]
        others.append(self.sibling())
        others.append(self.device(self.x, around(self.y, 2), self.z, 1 - self.c))
        for other in others:
            pl.semaphore_signal(barrier, inc=1, device_id=other, device_id_type=MESH)
        pl.semaphore_wait(barrier, len(others))


class Net:
    def __init__(self, place, sent, landed):
        self.place, self.sent, self.landed = place, sent, landed
        self.count = 0
        self.flying = {}

    def send(self, src, dst, device):
        slot = self.count
        self.count += 1
        copy = pltpu.make_async_remote_copy(
            src_ref=src,
            dst_ref=dst,
            send_sem=self.sent.at[slot],
            recv_sem=self.landed.at[slot],
            device_id=device,
            device_id_type=MESH,
        )
        copy.start()
        self.flying[slot] = copy
        return slot

    def wait(self, slot, dst):
        pltpu.make_async_remote_copy(
            src_ref=dst,
            dst_ref=dst,
            send_sem=self.sent.at[slot],
            recv_sem=self.landed.at[slot],
            device_id=self.place.sibling(),
            device_id_type=MESH,
        ).wait_recv()

    def gone(self, slots):
        for slot in slots:
            self.flying.pop(slot).wait_send()

    def drain(self):
        self.gone(list(self.flying))


class Gather:
    def __init__(self, net, place, full):
        self.net, self.place, self.full = net, place, full
        self.portion = full.shape[-1] // 3
        self.quarter = self.portion // 4

    def part_a(self, dy, dz):
        p = self.place
        y = around(p.y, 4 - dy)
        z = around(p.z, 4 - dz)
        return self.full.at[p.c, y, z, :, pl.ds(0, self.portion)]

    def part_b(self, dy, dz):
        p = self.place
        y = around(p.y, 4 - dy)
        z = around(p.z, 4 - dz)
        return self.full.at[p.c, y, z, :, pl.ds(self.portion, self.portion)]

    def columns(self, which, dx):
        x = around(self.place.x, 4 - dx)
        start = pl.multiple_of(which * self.portion + x * self.quarter, 128)
        return pl.ds(start, self.quarter)

    def quarter_b(self, dy, dx):
        p = self.place
        return self.full.at[p.c, around(p.y, 4 - dy), p.z, :, self.columns(1, dx)]

    def quarter_c(self, dy, dz, dx):
        p = self.place
        return self.full.at[
            p.c, around(p.y, 4 - dy), around(p.z, 4 - dz), :, self.columns(2, dx)
        ]

    def group_c(self, group, dx):
        p = self.place
        dy, dz = group
        if dz is None:
            return self.full.at[p.c, around(p.y, 4 - dy), :, :, self.columns(2, dx)]
        return self.quarter_c(dy, dz, dx)

    def share(self, name, c):
        p = self.place
        kind, shift = name
        if kind == "a":
            return self.full.at[c, around(p.y, 4 - shift), :, :, pl.ds(0, self.portion)]
        if kind == "b":
            return self.full.at[
                c, :, around(p.z, 4 - shift), :, pl.ds(self.portion, self.portion)
            ]
        return self.full.at[c, :, :, :, self.columns(2, shift)]

    def give(self, name):
        ref = self.share(name, self.place.c)
        self.shared.append((name, self.net.send(ref, ref, self.place.sibling())))

    def begin(self):
        net, p = self.net, self.place
        self.shared = []
        own_b, own_c = self.quarter_b(0, 0), self.quarter_c(0, 0, 0)
        own_a, own_whole_b = self.part_a(0, 0), self.part_b(0, 0)
        self.c_z, self.b_y, self.a_z = {}, {}, {}
        self.c_y, self.a_y, self.b_z = {}, {}, {}
        self.c_x, self.b_x = {}, {}
        for shift in (1, 3, 2):
            self.c_z[shift] = net.send(own_c, own_c, p.at("z", shift))
            self.b_y[shift] = net.send(own_b, own_b, p.at("y", shift))
        for shift in (1, 3, 2):
            self.a_z[shift] = net.send(own_a, own_a, p.at("z", shift))
            self.c_y[shift, 0] = net.send(own_c, own_c, p.at("y", shift))
        for shift in (1, 3):
            self.a_y[shift, 0] = net.send(own_a, own_a, p.at("y", shift))
            self.b_z[shift, 0] = net.send(own_whole_b, own_whole_b, p.at("z", shift))

    def second(self):
        net, p = self.net, self.place
        for d in (1, 3, 2):
            ref = self.quarter_c(0, d, 0)
            net.wait(self.c_z[d], ref)
            for shift in (1, 3, 2):
                self.c_y[shift, d] = net.send(ref, ref, p.at("y", shift))
            for shift in (1, 3):
                self.c_x[shift, (0, d)] = net.send(ref, ref, p.at("x", shift))
            ref = self.quarter_b(d, 0)
            net.wait(self.b_y[d], ref)
            for shift in (1, 3, 2):
                self.b_x[shift, d] = net.send(ref, ref, p.at("x", shift))
        for d in (1, 3, 2):
            ref = self.part_a(0, d)
            net.wait(self.a_z[d], ref)
            for shift in (1, 3):
                self.a_y[shift, d] = net.send(ref, ref, p.at("y", shift))
        self.give(("a", 0))

    def third(self):
        net, p = self.net, self.place
        for d in (1, 3, 2):
            for shift in (1, 3, 2):
                net.wait(self.b_x[shift, d], self.quarter_b(d, shift))
            ref = self.part_b(d, 0)
            for shift in (1, 3):
                self.b_z[shift, d] = net.send(ref, ref, p.at("z", shift))
            for dz in range(4):
                net.wait(self.c_y[d, dz], self.quarter_c(d, dz, 0))
            ref = self.group_c((d, None), 0)
            for shift in (1, 3):
                self.c_x[shift, (d, None)] = net.send(ref, ref, p.at("x", shift))
        self.give(("b", 0))
        self.give(("c", 0))

    def onward(self, table, keys, region, axis):
        net, p = self.net, self.place
        far = {}
        for number, key in enumerate(keys):
            for shift in (1, 3):
                ref = region(key, shift)
                net.wait(table[shift, key], ref)
                if (number % 2 == 0) == (shift == 1):
                    far[key] = net.send(ref, ref, p.at(axis, shift))
        return far

    def fourth(self):
        groups = [(0, 1), (0, 3), (0, 2), (1, None), (3, None), (2, None)]
        self.groups = groups
        self.a_far = self.onward(self.a_y, (0, 1, 3, 2), lambda d, s: self.part_a(s, d), "y")
        self.b_far = self.onward(self.b_z, (0, 1, 3, 2), lambda d, s: self.part_b(d, s), "z")
        self.c_far = self.onward(self.c_x, groups, lambda g, s: self.group_c(g, s), "x")
        for shift in (1, 3):
            for kind in "abc":
                self.give((kind, shift))

    def finish(self):
        net, p = self.net, self.place
        for d in (0, 1, 3, 2):
            net.wait(self.a_far[d], self.part_a(2, d))
        self.give(("a", 2))
        for d in (0, 1, 3, 2):
            net.wait(self.b_far[d], self.part_b(d, 2))
        self.give(("b", 2))
        for group in self.groups:
            net.wait(self.c_far[group], self.group_c(group, 2))
        self.give(("c", 2))
        for name, slot in self.shared:
            net.wait(slot, self.share(name, 1 - p.c))


GATHER_COPIES = 90


def add_into(target, term):
    target[...] = (target[...].astype(F32) + term[...].astype(F32)).astype(target.dtype)


class Scatter:
    def __init__(self, net, place, terms, bufs):
        self.net, self.place, self.terms = net, place, terms
        self.portion = terms.shape[-1] // 3
        self.quarter = self.portion // 4
        self.near, self.mid, self.final, self.done = bufs
        self.slots = {}

    @staticmethod
    def scratch(columns):
        portion, quarter = columns // 3, columns // 12
        return [
            [
                pltpu.VMEM((2, 2, ROWS, portion), BF16),
                pltpu.VMEM((2, 2, ROWS, portion), BF16),
                pltpu.VMEM((2, 2, 4, ROWS, quarter), BF16),
                pltpu.VMEM((2, 4, ROWS, portion), BF16),
                pltpu.VMEM((2, 4, ROWS, portion), BF16),
                pltpu.VMEM((2, 4, 4, ROWS, quarter), BF16),
            ],
            [
                pltpu.VMEM((3, ROWS, portion), BF16),
                pltpu.VMEM((3, 4, ROWS, quarter), BF16),
                pltpu.VMEM((3, 4, ROWS, quarter), BF16),
            ],
            [pltpu.VMEM((3, ROWS, quarter), BF16)] * 3,
            pltpu.VMEM((4, 3, ROWS, quarter), BF16),
        ]

    def columns(self, which, x):
        start = pl.multiple_of(which * self.portion + x * self.quarter, 128)
        return pl.ds(start, self.quarter)

    def whole(self, which):
        return pl.ds(which * self.portion, self.portion)

    def first(self, which, shift, half=None):
        p, of = self.place, self.terms
        part = slice(None) if half is None else pl.ds(2 * half, 2)
        if which == 0:
            return of.at[around(p.y, shift), part, :, self.whole(0)]
        if which == 1:
            return of.at[part, around(p.z, shift), :, self.whole(1)]
        return of.at[part, :, :, self.columns(2, around(p.x, shift))]

    def second(self, which, shift):
        p, mine = self.place, self.terms
        if which == 0:
            return mine.at[p.y, around(p.z, shift), :, self.whole(0)]
        if which == 1:
            return mine.at[:, p.z, :, self.columns(1, around(p.x, shift))]
        return mine.at[around(p.y, shift), :, :, self.columns(2, p.x)]

    def third(self, which, shift):
        p, mine = self.place, self.terms
        if which == 0:
            return mine.at[p.y, p.z, :, self.columns(0, around(p.x, shift))]
        if which == 1:
            return mine.at[around(p.y, shift), p.z, :, self.columns(1, p.x)]
        return mine.at[p.y, around(p.z, shift), :, self.columns(2, p.x)]

    AXES = (("y", "z", "x"), ("z", "x", "y"), ("x", "y", "z"))

    def step_far(self):
        net, p = self.net, self.place
        for which in range(3):
            axis = self.AXES[which][0]
            for half, shift in ((0, 1), (1, 3)):
                self.slots["far", which, half] = net.send(
                    self.first(which, 2, half),
                    self.near[which].at[half],
                    p.at(axis, shift),
                )

    def step_near(self):
        net, p = self.net, self.place
        for which in range(3):
            axis = self.AXES[which][0]
            for half, shift in ((0, 1), (1, 3)):
                came = self.near[which].at[half]
                net.wait(self.slots["far", which, half], came)
                target = self.first(which, shift, half)
                for i in range(2):
                    add_into(target.at[i], came.at[i])
                self.slots["near", which, half] = net.send(
                    self.first(which, shift),
                    self.near[3 + which].at[half],
                    p.at(axis, shift),
                )

    def step_second(self):
        net, p = self.net, self.place
        for which in range(3):
            axis = self.AXES[which][1]
            target = self.first(which, 0)
            for half in range(2):
                came = self.near[3 + which].at[half]
                net.wait(self.slots["near", which, half], came)
                for i in range(4):
                    add_into(target.at[i], came.at[i])
            for shift in (2, 1, 3):
                self.slots["second", which, shift] = net.send(
                    self.second(which, shift), self.mid[which].at[shift - 1], p.at(axis, shift)
                )

    def step_third(self):
        net, p = self.net, self.place
        for which in range(3):
            axis = self.AXES[which][2]
            target = self.second(which, 0)
            for shift in (1, 3, 2):
                came = self.mid[which].at[shift - 1]
                net.wait(self.slots["second", which, shift], came)
                if which == 0:
                    add_into(target, came)
                else:
                    for i in range(4):
                        add_into(target.at[i], came.at[i])
            for shift in (2, 1, 3):
                self.slots["third", which, shift] = net.send(
                    self.third(which, shift), self.final[which].at[shift - 1], p.at(axis, shift)
                )

    def step_spread(self):
        net, p = self.net, self.place
        for which in range(3):
            total = self.third(which, 0)[...].astype(F32)
            for shift in (1, 3, 2):
                came = self.final[which].at[shift - 1]
                net.wait(self.slots["third", which, shift], came)
                total = total + came[...].astype(F32)
            self.done[p.x, which] = total.astype(BF16)
        for shift in (2, 1, 3):
            self.slots["spread", shift] = net.send(
                self.done.at[p.x], self.done.at[p.x], p.at("x", shift)
            )

    def step_last(self, store):
        net, p = self.net, self.place
        for shift in (1, 3, 2):
            net.wait(self.slots["spread", shift], self.done.at[around(p.x, 4 - shift)])
        for which in range(3):
            for x in range(4):
                store(which * self.portion + x * self.quarter, self.done[x, which].astype(F32))


SCATTER_COPIES = 33


class Total:
    ORDERS = ("xyz", "yzx", "zxy")

    def __init__(self, net, place, terms, pair, stages, out):
        self.net, self.place, self.terms, self.pairbuf = net, place, terms, pair
        self.stages, self.out = stages, out
        self.slots = {}

    @staticmethod
    def scratch(rows, width):
        return [
            pltpu.VMEM((3, rows, width), F32),
            pltpu.VMEM((3, 3, 4, rows, width), F32),
        ]

    def coordinate(self, axis):
        return {"x": self.place.x, "y": self.place.y, "z": self.place.z}[axis]

    def to_sibling(self):
        p = self.place
        self.slots["pair"] = self.net.send(self.terms.at[1 - p.c], self.pairbuf, p.sibling())

    def put(self, stage, portion, value):
        axis = self.ORDERS[portion][stage]
        own = self.stages.at[stage, portion, self.coordinate(axis)]
        own[...] = value
        for shift in (2, 1, 3):
            self.slots[stage, portion, shift] = self.net.send(own, own, self.place.at(axis, shift))

    def begin(self):
        self.net.wait(self.slots["pair"], self.pairbuf)
        for portion in range(3):
            self.put(0, portion, self.terms[self.place.c, portion] + self.pairbuf[portion])

    def collect(self, stage, portion):
        axis = self.ORDERS[portion][stage]
        for shift in (1, 3, 2):
            other = around(self.coordinate(axis), 4 - shift)
            self.net.wait(self.slots[stage, portion, shift], self.stages.at[stage, portion, other])
        s = self.stages
        return (s[stage, portion, 0] + s[stage, portion, 1]) + (
            s[stage, portion, 2] + s[stage, portion, 3]
        )

    def step(self, stage):
        for portion in range(3):
            self.put(stage, portion, self.collect(stage - 1, portion))

    def spread(self):
        p = self.place
        for portion in range(3):
            self.out[p.c, portion] = self.collect(2, portion)
        self.slots["back"] = self.net.send(self.out.at[p.c], self.out.at[p.c], p.sibling())

    def last(self):
        self.net.wait(self.slots["back"], self.out.at[1 - self.place.c])


TOTAL_COPIES = 32


def swapped(value):
    return jnp.concatenate(
        [value[:, :384], value[:, 768:1152], value[:, 384:768], value[:, 1152:]], axis=1
    )


def rows_of(i, size):
    return pl.ds(pl.multiple_of(i * size, size), size)


def valid_rows(length, first, start, rows):
    position = first + start + lax.broadcasted_iota(jnp.int32, (rows, 1), 0)
    return (position < length).astype(F32)


def norm_stage(first, last, frames, gain, normed, mean_ref, inverse_ref):
    @pl.loop(first, last)
    def _(i):
        rows = rows_of(i, 32)
        value = frames[rows, :].astype(F32)
        mean = jnp.mean(value, -1, keepdims=True)
        center = value - mean
        inverse = lax.rsqrt(jnp.mean(center * center, -1, keepdims=True) + EPS)
        mean_ref[rows, :] = mean
        inverse_ref[rows, :] = inverse
        normed[rows, :] = swapped((center * inverse * gain[...]).astype(BF16))


def hidden_stage(first, last, normed, in_full, linear, opened, padded, valid):
    @pl.loop(first, last)
    def _(j):
        for half in range(2):
            rows = pl.ds(half * 256, 256)
            left = normed[rows, :]
            low = pl.ds(pl.multiple_of(j * 256, 256), 256)
            high = pl.ds(pl.multiple_of(D + j * 256, 256), 256)
            lin = jnp.dot(
                left, in_full[:, :, :, :, low].reshape(D, 256), preferred_element_type=F32
            )
            gate = jnp.dot(
                left, in_full[:, :, :, :, high].reshape(D, 256), preferred_element_type=F32
            )
            gate = jax.nn.sigmoid(gate)
            linear[rows, low] = lin.astype(BF16)
            opened[rows, low] = gate.astype(BF16)
            gated = (lin * gate * valid(half * 256, 256)).astype(BF16).astype(F32)
            inside = pl.ds(16 + half * 256, 256)
            padded[2 * j, inside, :] = gated[:, :128]
            padded[2 * j + 1, inside, :] = gated[:, 128:]


def taps_sum(source, i, base, tap):
    total = None
    for r in range(8):
        window = source[i, pl.ds(base + r + 1, 152), :]
        for j in range(4):
            k = 8 * j + r
            if k < 31:
                term = tap(k) * window[8 * j : 8 * j + 128]
                total = term if total is None else total + term
    return total


def conv_stage(bases, padded, taps, temporal):
    @pl.loop(0, 12)
    def _(i):
        for base in bases:
            total = taps_sum(padded, i, base, lambda k: taps[i, k : k + 1, :])
            temporal[pl.ds(base, 128), pl.ds(pl.multiple_of(i * 128, 128), 128)] = total


def mid_stage(temporal, gain, smooth_grad, smooth, grad_padded, mid_term):
    mid_term[...] = jnp.zeros_like(mid_term)

    @pl.loop(0, 16)
    def _(i):
        rows = rows_of(i, 32)
        value = temporal[rows, :]
        mean = jnp.mean(value, -1, keepdims=True)
        center = value - mean
        inverse = lax.rsqrt(jnp.mean(center * center, -1, keepdims=True) + EPS)
        hat = center * inverse
        scaled = hat * gain[...]
        s = jax.nn.sigmoid(scaled)
        smooth[rows, :] = swapped((scaled * s).astype(BF16))
        grad = smooth_grad[rows, :].astype(F32) * (s * (1.0 + scaled * (1.0 - s)))
        mid_term[...] += jnp.sum((grad * hat).reshape(4, 8, D), 0)
        q = grad * gain[...]
        result = inverse * (
            q - jnp.mean(q, -1, keepdims=True) - hat * jnp.mean(q * hat, -1, keepdims=True)
        )
        result = result.astype(BF16).astype(F32)
        inside = pl.ds(pl.multiple_of(16 + i * 32, 16), 32)
        for t in range(12):
            grad_padded[t, inside, :] = result[:, t * 128 : (t + 1) * 128]


def backward_conv(first, last, padded, grad_padded, taps, linear, opened, valid, hidden_grad, sums):
    @pl.loop(first, last)
    def _(i):
        columns = pl.ds(pl.multiple_of(i * 128, 128), 128)
        high = pl.ds(pl.multiple_of(D + i * 128, 128), 128)
        for base in range(0, 512, 128):
            rows = pl.ds(base, 128)
            grad = taps_sum(grad_padded, i, base, lambda k: taps[i, 30 - k : 31 - k, :])
            grad = grad * valid(base, 128)
            gate = opened[rows, columns].astype(F32)
            direct = grad * gate
            hidden_grad[rows, columns] = direct.astype(BF16)
            hidden_grad[rows, high] = (
                direct * linear[rows, columns].astype(F32) * (1.0 - gate)
            ).astype(BF16)
            here = grad_padded[i, pl.ds(base + 16, 128), :]
            for r in range(8):
                window = padded[i, pl.ds(base + r + 1, 152), :]
                for j in range(4):
                    k = 8 * j + r
                    if k < 31:
                        term = (window[8 * j : 8 * j + 128] * here).reshape(16, 8, 128)
                        term = jnp.sum(term, 0)
                        if base:
                            sums[i, k] += term
                        else:
                            sums[i, k] = term


def transposed_product(left, right):
    return lax.dot_general(
        left, right, (((1,), (1,)), ((), ())), preferred_element_type=F32
    )


def transpose_stage(source, own, other, c):
    for half, target in ((c, own), (1 - c, other)):

        @pl.loop(0, 6)
        def _(j):
            columns = pl.ds(pl.multiple_of(half * HALF + j * 128, 128), 128)
            for base in range(0, FRAMES, 128):
                block = source[pl.ds(base, 128), columns]
                target[rows_of(j, 128), pl.ds(base, 128)] = jnp.transpose(block)


def weight_grad(left, right, right_column, target, target_column):
    @pl.loop(0, 6)
    def _(t):
        value = jnp.dot(
            left[...],
            right[:, pl.ds(pl.multiple_of(right_column(t), 256), 256)],
            preferred_element_type=F32,
        )
        target[:, :, :, pl.ds(pl.multiple_of(target_column(t), 256), 256)] = (
            value.astype(BF16).reshape(4, 4, ROWS, 256)
        )


def back_product(parts, left, full, result):
    for q in parts:
        yh, c = q // 2, q % 2
        weights = full[c, 2 * yh : 2 * yh + 2].reshape(384, full.shape[-1])
        result[:, q * 384 : (q + 1) * 384] = transposed_product(left[...], weights).astype(
            result.dtype
        )


def branch_stage(smooth, out_full, frames, valid, mixed):
    @pl.loop(0, 6)
    def _(j):
        columns = rows_of(j, 256)
        value = jnp.dot(
            smooth[...],
            out_full[:, :, :, :, columns].reshape(D, 256),
            preferred_element_type=F32,
        )
        mixed[:, columns] = (frames[:, columns].astype(F32) + valid(0, 512) * value).astype(BF16)


def frames_stage(frames, cotangent, gain, mean_ref, inverse_ref, normed_grad, result, in_term):
    in_term[...] = jnp.zeros_like(in_term)

    @pl.loop(0, 16)
    def _(i):
        rows = rows_of(i, 32)
        inverse = inverse_ref[rows, :]
        centred = (frames[rows, :].astype(F32) - mean_ref[rows, :]) * inverse
        grad = normed_grad[rows, :]
        in_term[...] += jnp.sum((grad * centred).reshape(4, 8, D), 0)
        p = grad * gain[...]
        change = inverse * (
            p - jnp.mean(p, -1, keepdims=True) - centred * jnp.mean(p * centred, -1, keepdims=True)
        )
        result[rows, :] = (cotangent[rows, :].astype(F32) + change).astype(BF16)


def edges(net, place, padded):
    tm = lax.axis_index("tm")
    rows = {"first": padded.at[:, 16:32, :], "last": padded.at[:, FRAMES : FRAMES + 16, :]}
    before, after = padded.at[:, 0:16, :], padded.at[:, FRAMES + 16 : FRAMES + 32, :]
    here = (lax.axis_index("utt"), lax.axis_index("wshard"))
    ahead = (here[0], around(tm, 1), here[1])
    behind = (here[0], around(tm, 3), here[1])
    slots = (net.send(rows["last"], before, ahead), net.send(rows["first"], after, behind))

    def arrive():
        net.wait(slots[0], before)
        net.wait(slots[1], after)
        padded[:, 0:16, :] = padded[:, 0:16, :] * (tm > 0).astype(F32)
        padded[:, FRAMES + 16 : FRAMES + 32, :] = padded[:, FRAMES + 16 : FRAMES + 32, :] * (
            tm < 3
        ).astype(F32)

    return arrive


def module_kernel(scale, tree, *refs):
    (
        length_ref, frames_hbm, cotangent_hbm, norm_gain, in_hbm, taps, mid_gain, out_hbm,
        mixed_hbm, grad_frames_hbm, grad_in, grad_out, grad_taps, grad_norm_gain, grad_mid_gain,
    ) = refs[:15]
    (
        in_full, out_full, frames, branch_grad, normed, smooth, linear, opened, padded, grad_padded,
        temporal, smooth_grad, hidden_grad, normed_t, smooth_t, other_t, mean_ref, inverse_ref,
        sums, mid_term, in_term, first_terms, second_terms, small, small_sum,
        sent, landed, local, bufs,
    ) = jax.tree_util.tree_unflatten(tree, refs[15:])
    place = Place()
    net = Net(place, sent, landed)
    c = place.c
    sibling = place.sibling()
    length = length_ref[0]
    start = lax.axis_index("tm") * FRAMES

    def valid(first, rows):
        return valid_rows(length, start, first, rows)

    loads = [
        pltpu.make_async_copy(in_hbm, in_full.at[c, place.y, place.z], local.at[0]),
        pltpu.make_async_copy(frames_hbm, frames, local.at[1]),
        pltpu.make_async_copy(cotangent_hbm, branch_grad.at[0:FRAMES], local.at[2]),
        pltpu.make_async_copy(out_hbm, out_full.at[c, place.y, place.z], local.at[3]),
    ]
    for load in loads:
        load.start()
    place.greet()
    gather_in, gather_out = Gather(net, place, in_full), Gather(net, place, out_full)
    loads[0].wait()
    gather_in.begin()
    loads[1].wait()
    norm = (frames, norm_gain, normed, mean_ref, inverse_ref)
    norm_stage(0, 6, *norm)
    gather_in.second()
    norm_stage(6, 16, *norm)
    gather_in.third()
    loads[2].wait()

    @pl.loop(0, 8)
    def _(i):
        rows = rows_of(i, 64)
        branch_grad[rows, :] = (branch_grad[rows, :].astype(F32) * valid(i * 64, 64)).astype(BF16)

    pair_branch = net.send(branch_grad.at[0:FRAMES], branch_grad.at[FRAMES : 2 * FRAMES], sibling)
    transpose_stage(normed, normed_t.at[:, 0:FRAMES], other_t, c)
    pair_normed = net.send(other_t, normed_t.at[:, FRAMES : 2 * FRAMES], sibling)
    gather_in.fourth()
    loads[3].wait()
    out_first = net.count
    gather_out.begin()
    gather_in.finish()
    gather_out.second()
    hidden = (normed, in_full, linear, opened, padded, valid)
    hidden_stage(0, 3, *hidden)
    gather_out.third()
    hidden_stage(3, 6, *hidden)
    arrive = edges(net, place, padded)
    gather_out.fourth()
    conv_stage((128, 256), padded, taps, temporal)
    arrive()
    conv_stage((0, 384), padded, taps, temporal)
    gather_out.finish()
    out_last = net.count
    back_product(range(4), branch_grad.at[0:FRAMES], out_full, smooth_grad)
    mid_stage(temporal, mid_gain, smooth_grad, smooth, grad_padded, mid_term)
    arrive = edges(net, place, grad_padded)

    net.gone([pair_normed])
    transpose_stage(smooth, smooth_t.at[:, 0:FRAMES], other_t, c)
    pair_smooth = net.send(other_t, smooth_t.at[:, FRAMES : 2 * FRAMES], sibling)
    arrive()
    conv = (padded, grad_padded, taps, linear, opened, valid, hidden_grad, sums)
    pair_hidden = []

    def backward(group):
        backward_conv(2 * group, 2 * group + 2, *conv)
        for column in (256 * group, D + 256 * group):
            own = hidden_grad.at[0:FRAMES, column : column + 256]
            there = hidden_grad.at[FRAMES : 2 * FRAMES, column : column + 256]
            pair_hidden.append((net.send(own, there, sibling), there))

    def hidden_arrive():
        while pair_hidden:
            net.wait(*pair_hidden.pop(0))

    backward(0)
    net.wait(pair_branch, branch_grad.at[FRAMES : 2 * FRAMES])
    net.wait(pair_smooth, smooth_t.at[:, FRAMES : 2 * FRAMES])
    weight_grad(smooth_t, branch_grad, lambda t: t * 256, first_terms, lambda t: t * 256)
    scatter_out = Scatter(net, place, first_terms, bufs[0])
    scatter_out.step_far()
    backward(1)
    backward(2)
    scatter_out.step_near()
    net.wait(pair_normed, normed_t.at[:, FRAMES : 2 * FRAMES])
    hidden_arrive()

    def grad_half(half, target):
        weight_grad(
            normed_t,
            hidden_grad,
            lambda t: lax.rem(t, 2) * D + half * HALF + lax.div(t, 2) * 256,
            target,
            lambda t: lax.rem(t, 2) * HALF + lax.div(t, 2) * 256,
        )

    grad_half(0, second_terms)
    scatter_one = Scatter(net, place, second_terms, bufs[1])
    scatter_one.step_far()
    scatter_out.step_second()
    backward(3)
    scatter_out.step_third()
    backward(4)
    scatter_one.step_near()
    backward(5)
    scatter_out.step_spread()
    branch_stage(smooth, out_full, frames, valid, normed)
    store_mixed = pltpu.make_async_copy(normed, mixed_hbm, local.at[0])
    store_mixed.start()
    scatter_one.step_second()
    hidden_arrive()
    net.gone(range(out_first, out_last))
    third_terms = out_full.at[0]
    grad_half(1, third_terms)
    scatter_two = Scatter(net, place, third_terms, bufs[2])
    scatter_two.step_far()
    scatter_one.step_third()
    reload = pltpu.make_async_copy(cotangent_hbm, opened, local.at[1])
    reload.start()

    def store_out(column, value):
        grad_out[:, column : column + 128] = value * scale

    def store_in(half):
        def store(column, value):
            to = half * HALF + column + (HALF if column >= HALF else 0)
            grad_in[:, to : to + 128] = value * scale

        return store

    own_hidden = hidden_grad.at[0:FRAMES]
    back_product((0, 1), own_hidden, in_full, temporal)
    scatter_two.step_near()
    back_product((2, 3), own_hidden, in_full, temporal)
    scatter_two.step_second()
    reload.wait()
    frames_stage(
        frames, opened, norm_gain, mean_ref, inverse_ref, temporal, smooth, in_term
    )
    store_frames = pltpu.make_async_copy(smooth, grad_frames_hbm, local.at[2])
    store_frames.start()
    for i in range(12):
        lanes = slice((i % 2) * 128, (i % 2) * 128 + 128)
        columns = slice(i * 128, i * 128 + 128)
        core, portion = (i // 2) % 2, i // 4
        small[core, portion, 0:31, lanes] = jnp.sum(sums[i], 1)[0:31]
        small[core, portion, 31:32, lanes] = jnp.sum(in_term[:, columns], 0, keepdims=True)
        small[core, portion, 32:33, lanes] = jnp.sum(mid_term[:, columns], 0, keepdims=True)
        small[core, portion, 33:40, lanes] = jnp.zeros((7, 128), F32)
    total = Total(net, place, small, *bufs[3], small_sum)
    total.to_sibling()
    scatter_two.step_third()
    total.begin()
    scatter_one.step_spread()
    scatter_out.step_last(store_out)
    total.step(1)
    scatter_two.step_spread()
    total.step(2)
    scatter_one.step_last(store_in(0))
    total.spread()
    scatter_two.step_last(store_in(1))
    total.last()
    for core in range(2):
        for portion in range(3):
            columns = slice(portion * 512 + core * 256, portion * 512 + core * 256 + 256)
            grad_taps[:, columns] = small_sum[core, portion, 0:31, :] * scale
            grad_norm_gain[:, columns] = small_sum[core, portion, 31:32, :] * scale
            grad_mid_gain[:, columns] = small_sum[core, portion, 32:33, :] * scale
    store_mixed.wait()
    store_frames.wait()
    net.drain()


def body(frames, lengths, cotangent, norm_gain, w_in, kernel, mid_gain, w_out):
    scale = 1.0 / math.sqrt(
        FRAMES * lax.axis_size("utt") * lax.axis_size("tm") * lax.axis_size("wshard")
    )
    taps = jnp.pad(kernel, ((0, 1), (0, 0))).reshape(32, 12, 128).swapaxes(0, 1)
    block = (FRAMES, D)
    copies = 2 * GATHER_COPIES + 3 * SCATTER_COPIES + TOTAL_COPIES + 32
    scratch = [
        pltpu.VMEM((2, 4, 4, ROWS, 2 * D), BF16),
        pltpu.VMEM((2, 4, 4, ROWS, D), BF16),
        pltpu.VMEM(block, BF16),
        pltpu.VMEM((2 * FRAMES, D), BF16),
        pltpu.VMEM(block, BF16),
        pltpu.VMEM(block, BF16),
        pltpu.VMEM(block, BF16),
        pltpu.VMEM(block, BF16),
        pltpu.VMEM((12, FRAMES + 32, 128), F32),
        pltpu.VMEM((12, FRAMES + 32, 128), F32),
        pltpu.VMEM(block, F32),
        pltpu.VMEM(block, BF16),
        pltpu.VMEM((2 * FRAMES, 2 * D), BF16),
        pltpu.VMEM((HALF, 2 * FRAMES), BF16),
        pltpu.VMEM((HALF, 2 * FRAMES), BF16),
        pltpu.VMEM((HALF, FRAMES), BF16),
        pltpu.VMEM((FRAMES, 1), F32),
        pltpu.VMEM((FRAMES, 1), F32),
        pltpu.VMEM((12, 32, 8, 128), F32),
        pltpu.VMEM((8, D), F32),
        pltpu.VMEM((8, D), F32),
        pltpu.VMEM((4, 4, ROWS, D), BF16),
        pltpu.VMEM((4, 4, ROWS, D), BF16),
        pltpu.VMEM((2, 3, 40, 256), F32),
        pltpu.VMEM((2, 3, 40, 256), F32),
        pltpu.SemaphoreType.DMA((copies,)),
        pltpu.SemaphoreType.DMA((copies,)),
        pltpu.SemaphoreType.DMA((4,)),
        [Scatter.scratch(D), Scatter.scratch(D), Scatter.scratch(D), Total.scratch(40, 256)],
    ]
    leaves, tree = jax.tree_util.tree_flatten(scratch)
    anywhere = pl.BlockSpec(memory_space=pl.ANY)
    inside = pl.BlockSpec(memory_space=pltpu.VMEM)
    scalar = pl.BlockSpec(memory_space=pltpu.SMEM)
    outs = pl.pallas_call(
        functools.partial(module_kernel, scale, tree),
        out_shape=[
            jax.ShapeDtypeStruct(block, BF16),
            jax.ShapeDtypeStruct(block, BF16),
            jax.ShapeDtypeStruct((ROWS, 2 * D), F32),
            jax.ShapeDtypeStruct((ROWS, D), F32),
            jax.ShapeDtypeStruct((31, D), F32),
            jax.ShapeDtypeStruct((1, D), F32),
            jax.ShapeDtypeStruct((1, D), F32),
        ],
        in_specs=[scalar, anywhere, anywhere, inside, anywhere, inside, inside, anywhere],
        out_specs=[anywhere, anywhere, inside, inside, inside, inside, inside],
        scratch_shapes=leaves,
        compiler_params=pltpu.CompilerParams(
            collective_id=0, has_side_effects=True, vmem_limit_bytes=63 * 2**20
        ),
    )(
        lengths, frames[0], cotangent[0], norm_gain[None], w_in, taps, mid_gain[None], w_out
    )
    mixed, grad_frames, grad_in, grad_out, grad_taps, grad_norm_gain, grad_mid_gain = outs
    return (
        mixed[None], grad_frames[None], grad_in, grad_out,
        grad_taps, grad_norm_gain[0], grad_mid_gain[0],
    )


def solution(mesh):
    return jax.shard_map(
        body,
        mesh=mesh,
        in_specs=(
            P(("utt", "wshard"), "tm", None),
            P(("utt", "wshard")),
            P(("utt", "wshard"), "tm", None),
            P(),
            P(("tm", "wshard"), None),
            P(),
            P(),
            P(("tm", "wshard"), None),
        ),
        out_specs=(
            P(("utt", "wshard"), "tm", None),
            P(("utt", "wshard"), "tm", None),
            P(("tm", "wshard"), None),
            P(("tm", "wshard"), None),
            P(),
            P(),
            P(),
        ),
        check_vma=False,
    )
```

```python
import functools
import math

import jax
import jax.numpy as jnp
from jax import lax
from jax.experimental import pallas as pl
from jax.experimental.pallas import tpu as pltpu
from jax.sharding import PartitionSpec as P

EPS = 1e-05
MESH = pl.DeviceIdType.MESH
F32 = jnp.float32
BF16 = jnp.bfloat16
ROWS = 48
D = 1536
FRAMES = 512
HALF = D // 2


def around(value, shift):
    return lax.rem(value + shift, 4)


class Place:
    def __init__(self):
        tm, ws = lax.axis_index("tm"), lax.axis_index("wshard")
        self.x = lax.axis_index("utt")
        self.c = lax.rem(tm, 2)
        self.y = lax.div(tm, 2) * 2 + lax.div(ws, 4)
        self.z = lax.rem(ws, 4)

    def device(self, x, y, z, c):
        return (x, lax.div(y, 2) * 2 + c, lax.rem(y, 2) * 4 + z)

    def at(self, axis, shift):
        x, y, z = self.x, self.y, self.z
        if axis == "x":
            x = around(x, shift)
        if axis == "y":
            y = around(y, shift)
        if axis == "z":
            z = around(z, shift)
        return self.device(x, y, z, self.c)

    def sibling(self):
        return self.device(self.x, self.y, self.z, 1 - self.c)

    def greet(self):
        barrier = pltpu.get_barrier_semaphore()
        others = [self.at(axis, shift) for axis in "xyz" for shift in (1, 2, 3)]
        others.append(self.sibling())
        others.append(self.device(self.x, around(self.y, 2), self.z, 1 - self.c))
        for other in others:
            pl.semaphore_signal(barrier, inc=1, device_id=other, device_id_type=MESH)
        pl.semaphore_wait(barrier, len(others))


class Net:
    def __init__(self, place, sent, landed):
        self.place, self.sent, self.landed = place, sent, landed
        self.count = 0
        self.flying = {}

    def send(self, src, dst, device):
        slot = self.count
        self.count += 1
        copy = pltpu.make_async_remote_copy(
            src_ref=src,
            dst_ref=dst,
            send_sem=self.sent.at[slot],
            recv_sem=self.landed.at[slot],
            device_id=device,
            device_id_type=MESH,
        )
        copy.start()
        self.flying[slot] = copy
        return slot

    def wait(self, slot, dst):
        pltpu.make_async_remote_copy(
            src_ref=dst,
            dst_ref=dst,
            send_sem=self.sent.at[slot],
            recv_sem=self.landed.at[slot],
            device_id=self.place.sibling(),
            device_id_type=MESH,
        ).wait_recv()

    def gone(self, slots):
        for slot in slots:
            self.flying.pop(slot).wait_send()

    def drain(self):
        self.gone(list(self.flying))


class Gather:
    def __init__(self, net, place, full):
        self.net, self.place, self.full = net, place, full
        self.portion = full.shape[-1] // 3
        self.quarter = self.portion // 4

    def part_a(self, dy, dz):
        p = self.place
        y = around(p.y, 4 - dy)
        z = around(p.z, 4 - dz)
        return self.full.at[p.c, y, z, :, pl.ds(0, self.portion)]

    def part_b(self, dy, dz):
        p = self.place
        y = around(p.y, 4 - dy)
        z = around(p.z, 4 - dz)
        return self.full.at[p.c, y, z, :, pl.ds(self.portion, self.portion)]

    def columns(self, which, dx):
        x = around(self.place.x, 4 - dx)
        start = pl.multiple_of(which * self.portion + x * self.quarter, 128)
        return pl.ds(start, self.quarter)

    def quarter_b(self, dy, dx):
        p = self.place
        return self.full.at[p.c, around(p.y, 4 - dy), p.z, :, self.columns(1, dx)]

    def quarter_c(self, dy, dz, dx):
        p = self.place
        return self.full.at[
            p.c, around(p.y, 4 - dy), around(p.z, 4 - dz), :, self.columns(2, dx)
        ]

    def group_c(self, group, dx):
        p = self.place
        dy, dz = group
        if dz is None:
            return self.full.at[p.c, around(p.y, 4 - dy), :, :, self.columns(2, dx)]
        return self.quarter_c(dy, dz, dx)

    def share(self, name, c):
        p = self.place
        kind, shift = name
        if kind == "a":
            return self.full.at[c, around(p.y, 4 - shift), :, :, pl.ds(0, self.portion)]
        if kind == "b":
            return self.full.at[
                c, :, around(p.z, 4 - shift), :, pl.ds(self.portion, self.portion)
            ]
        return self.full.at[c, :, :, :, self.columns(2, shift)]

    def give(self, name):
        ref = self.share(name, self.place.c)
        self.shared.append((name, self.net.send(ref, ref, self.place.sibling())))

    def begin(self):
        net, p = self.net, self.place
        self.shared = []
        own_b, own_c = self.quarter_b(0, 0), self.quarter_c(0, 0, 0)
        own_a, own_whole_b = self.part_a(0, 0), self.part_b(0, 0)
        self.c_z, self.b_y, self.a_z = {}, {}, {}
        self.c_y, self.a_y, self.b_z = {}, {}, {}
        self.c_x, self.b_x = {}, {}
        for shift in (1, 3, 2):
            self.c_z[shift] = net.send(own_c, own_c, p.at("z", shift))
            self.b_y[shift] = net.send(own_b, own_b, p.at("y", shift))
        for shift in (1, 3, 2):
            self.a_z[shift] = net.send(own_a, own_a, p.at("z", shift))
            self.c_y[shift, 0] = net.send(own_c, own_c, p.at("y", shift))
        for shift in (1, 3):
            self.a_y[shift, 0] = net.send(own_a, own_a, p.at("y", shift))
            self.b_z[shift, 0] = net.send(own_whole_b, own_whole_b, p.at("z", shift))

    def second(self):
        net, p = self.net, self.place
        for d in (1, 3, 2):
            ref = self.quarter_c(0, d, 0)
            net.wait(self.c_z[d], ref)
            for shift in (1, 3, 2):
                self.c_y[shift, d] = net.send(ref, ref, p.at("y", shift))
            for shift in (1, 3):
                self.c_x[shift, (0, d)] = net.send(ref, ref, p.at("x", shift))
            ref = self.quarter_b(d, 0)
            net.wait(self.b_y[d], ref)
            for shift in (1, 3, 2):
                self.b_x[shift, d] = net.send(ref, ref, p.at("x", shift))
        for d in (1, 3, 2):
            ref = self.part_a(0, d)
            net.wait(self.a_z[d], ref)
            for shift in (1, 3):
                self.a_y[shift, d] = net.send(ref, ref, p.at("y", shift))
        self.give(("a", 0))

    def third(self):
        net, p = self.net, self.place
        for d in (1, 3, 2):
            for shift in (1, 3, 2):
                net.wait(self.b_x[shift, d], self.quarter_b(d, shift))
            ref = self.part_b(d, 0)
            for shift in (1, 3):
                self.b_z[shift, d] = net.send(ref, ref, p.at("z", shift))
            for dz in range(4):
                net.wait(self.c_y[d, dz], self.quarter_c(d, dz, 0))
            ref = self.group_c((d, None), 0)
            for shift in (1, 3):
                self.c_x[shift, (d, None)] = net.send(ref, ref, p.at("x", shift))
        self.give(("b", 0))
        self.give(("c", 0))

    def onward(self, table, keys, region, axis):
        net, p = self.net, self.place
        far = {}
        for number, key in enumerate(keys):
            for shift in (1, 3):
                ref = region(key, shift)
                net.wait(table[shift, key], ref)
                if (number % 2 == 0) == (shift == 1):
                    far[key] = net.send(ref, ref, p.at(axis, shift))
        return far

    def fourth(self):
        groups = [(0, 1), (0, 3), (0, 2), (1, None), (3, None), (2, None)]
        self.groups = groups
        self.a_far = self.onward(self.a_y, (0, 1, 3, 2), lambda d, s: self.part_a(s, d), "y")
        self.b_far = self.onward(self.b_z, (0, 1, 3, 2), lambda d, s: self.part_b(d, s), "z")
        self.c_far = self.onward(self.c_x, groups, lambda g, s: self.group_c(g, s), "x")
        for shift in (1, 3):
            for kind in "abc":
                self.give((kind, shift))

    def finish(self):
        net, p = self.net, self.place
        for d in (0, 1, 3, 2):
            net.wait(self.a_far[d], self.part_a(2, d))
        self.give(("a", 2))
        for d in (0, 1, 3, 2):
            net.wait(self.b_far[d], self.part_b(d, 2))
        self.give(("b", 2))
        for group in self.groups:
            net.wait(self.c_far[group], self.group_c(group, 2))
        self.give(("c", 2))
        for name, slot in self.shared:
            net.wait(slot, self.share(name, 1 - p.c))


GATHER_COPIES = 90


def add_into(target, term):
    target[...] = (target[...].astype(F32) + term[...].astype(F32)).astype(target.dtype)


class Scatter:
    def __init__(self, net, place, terms, bufs):
        self.net, self.place, self.terms = net, place, terms
        self.portion = terms.shape[-1] // 3
        self.quarter = self.portion // 4
        self.near, self.mid, self.final, self.done = bufs
        self.slots = {}

    @staticmethod
    def scratch(columns):
        portion, quarter = columns // 3, columns // 12
        return [
            [
                pltpu.VMEM((2, 2, ROWS, portion), BF16),
                pltpu.VMEM((2, 2, ROWS, portion), BF16),
                pltpu.VMEM((2, 2, 4, ROWS, quarter), BF16),
                pltpu.VMEM((2, 4, ROWS, portion), BF16),
                pltpu.VMEM((2, 4, ROWS, portion), BF16),
                pltpu.VMEM((2, 4, 4, ROWS, quarter), BF16),
            ],
            [
                pltpu.VMEM((3, ROWS, portion), BF16),
                pltpu.VMEM((3, 4, ROWS, quarter), BF16),
                pltpu.VMEM((3, 4, ROWS, quarter), BF16),
            ],
            [pltpu.VMEM((3, ROWS, quarter), BF16)] * 3,
            pltpu.VMEM((4, 3, ROWS, quarter), BF16),
        ]

    def columns(self, which, x):
        start = pl.multiple_of(which * self.portion + x * self.quarter, 128)
        return pl.ds(start, self.quarter)

    def whole(self, which):
        return pl.ds(which * self.portion, self.portion)

    def first(self, which, shift, half=None):
        p, of = self.place, self.terms
        part = slice(None) if half is None else pl.ds(2 * half, 2)
        if which == 0:
            return of.at[around(p.y, shift), part, :, self.whole(0)]
        if which == 1:
            return of.at[part, around(p.z, shift), :, self.whole(1)]
        return of.at[part, :, :, self.columns(2, around(p.x, shift))]

    def second(self, which, shift):
        p, mine = self.place, self.terms
        if which == 0:
            return mine.at[p.y, around(p.z, shift), :, self.whole(0)]
        if which == 1:
            return mine.at[:, p.z, :, self.columns(1, around(p.x, shift))]
        return mine.at[around(p.y, shift), :, :, self.columns(2, p.x)]

    def third(self, which, shift):
        p, mine = self.place, self.terms
        if which == 0:
            return mine.at[p.y, p.z, :, self.columns(0, around(p.x, shift))]
        if which == 1:
            return mine.at[around(p.y, shift), p.z, :, self.columns(1, p.x)]
        return mine.at[p.y, around(p.z, shift), :, self.columns(2, p.x)]

    AXES = (("y", "z", "x"), ("z", "x", "y"), ("x", "y", "z"))

    def step_far(self):
        net, p = self.net, self.place
        for which in range(3):
            axis = self.AXES[which][0]
            for half, shift in ((0, 1), (1, 3)):
                self.slots["far", which, half] = net.send(
                    self.first(which, 2, half),
                    self.near[which].at[half],
                    p.at(axis, shift),
                )

    def step_near(self):
        net, p = self.net, self.place
        for which in range(3):
            axis = self.AXES[which][0]
            for half, shift in ((0, 1), (1, 3)):
                came = self.near[which].at[half]
                net.wait(self.slots["far", which, half], came)
                target = self.first(which, shift, half)
                for i in range(2):
                    add_into(target.at[i], came.at[i])
                self.slots["near", which, half] = net.send(
                    self.first(which, shift),
                    self.near[3 + which].at[half],
                    p.at(axis, shift),
                )

    def step_second(self):
        net, p = self.net, self.place
        for which in range(3):
            axis = self.AXES[which][1]
            target = self.first(which, 0)
            for half in range(2):
                came = self.near[3 + which].at[half]
                net.wait(self.slots["near", which, half], came)
                for i in range(4):
                    add_into(target.at[i], came.at[i])
            for shift in (2, 1, 3):
                self.slots["second", which, shift] = net.send(
                    self.second(which, shift), self.mid[which].at[shift - 1], p.at(axis, shift)
                )

    def step_third(self):
        net, p = self.net, self.place
        for which in range(3):
            axis = self.AXES[which][2]
            target = self.second(which, 0)
            for shift in (1, 3, 2):
                came = self.mid[which].at[shift - 1]
                net.wait(self.slots["second", which, shift], came)
                if which == 0:
                    add_into(target, came)
                else:
                    for i in range(4):
                        add_into(target.at[i], came.at[i])
            for shift in (2, 1, 3):
                self.slots["third", which, shift] = net.send(
                    self.third(which, shift), self.final[which].at[shift - 1], p.at(axis, shift)
                )

    def step_spread(self):
        net, p = self.net, self.place
        for which in range(3):
            total = self.third(which, 0)[...].astype(F32)
            for shift in (1, 3, 2):
                came = self.final[which].at[shift - 1]
                net.wait(self.slots["third", which, shift], came)
                total = total + came[...].astype(F32)
            self.done[p.x, which] = total.astype(BF16)
        for shift in (2, 1, 3):
            self.slots["spread", shift] = net.send(
                self.done.at[p.x], self.done.at[p.x], p.at("x", shift)
            )

    def step_last(self, store):
        net, p = self.net, self.place
        for shift in (1, 3, 2):
            net.wait(self.slots["spread", shift], self.done.at[around(p.x, 4 - shift)])
        for which in range(3):
            for x in range(4):
                store(which * self.portion + x * self.quarter, self.done[x, which].astype(F32))


SCATTER_COPIES = 33


class Total:
    ORDERS = ("xyz", "yzx", "zxy")

    def __init__(self, net, place, terms, pair, stages, out):
        self.net, self.place, self.terms, self.pairbuf = net, place, terms, pair
        self.stages, self.out = stages, out
        self.slots = {}

    @staticmethod
    def scratch(rows, width):
        return [
            pltpu.VMEM((3, rows, width), F32),
            pltpu.VMEM((3, 3, 4, rows, width), F32),
        ]

    def coordinate(self, axis):
        return {"x": self.place.x, "y": self.place.y, "z": self.place.z}[axis]

    def to_sibling(self):
        p = self.place
        self.slots["pair"] = self.net.send(self.terms.at[1 - p.c], self.pairbuf, p.sibling())

    def put(self, stage, portion, value):
        axis = self.ORDERS[portion][stage]
        own = self.stages.at[stage, portion, self.coordinate(axis)]
        own[...] = value
        for shift in (2, 1, 3):
            self.slots[stage, portion, shift] = self.net.send(own, own, self.place.at(axis, shift))

    def begin(self):
        self.net.wait(self.slots["pair"], self.pairbuf)
        for portion in range(3):
            self.put(0, portion, self.terms[self.place.c, portion] + self.pairbuf[portion])

    def collect(self, stage, portion):
        axis = self.ORDERS[portion][stage]
        for shift in (1, 3, 2):
            other = around(self.coordinate(axis), 4 - shift)
            self.net.wait(self.slots[stage, portion, shift], self.stages.at[stage, portion, other])
        s = self.stages
        return (s[stage, portion, 0] + s[stage, portion, 1]) + (
            s[stage, portion, 2] + s[stage, portion, 3]
        )

    def step(self, stage):
        for portion in range(3):
            self.put(stage, portion, self.collect(stage - 1, portion))

    def spread(self):
        p = self.place
        for portion in range(3):
            self.out[p.c, portion] = self.collect(2, portion)
        self.slots["back"] = self.net.send(self.out.at[p.c], self.out.at[p.c], p.sibling())

    def last(self):
        self.net.wait(self.slots["back"], self.out.at[1 - self.place.c])


TOTAL_COPIES = 32


def swapped(value):
    return jnp.concatenate(
        [value[:, :384], value[:, 768:1152], value[:, 384:768], value[:, 1152:]], axis=1
    )


def rows_of(i, size):
    return pl.ds(pl.multiple_of(i * size, size), size)


def valid_rows(length, first, start, rows):
    position = first + start + lax.broadcasted_iota(jnp.int32, (rows, 1), 0)
    return (position < length).astype(F32)


def norm_stage(first, last, frames, gain, normed, mean_ref, inverse_ref):
    @pl.loop(first, last)
    def _(i):
        rows = rows_of(i, 32)
        value = frames[rows, :].astype(F32)
        mean = jnp.mean(value, -1, keepdims=True)
        center = value - mean
        inverse = lax.rsqrt(jnp.mean(center * center, -1, keepdims=True) + EPS)
        mean_ref[rows, :] = mean
        inverse_ref[rows, :] = inverse
        normed[rows, :] = swapped((center * inverse * gain[...]).astype(BF16))


def hidden_stage(first, last, normed, in_full, linear, opened, padded, valid):
    @pl.loop(first, last)
    def _(j):
        for half in range(2):
            rows = pl.ds(half * 256, 256)
            left = normed[rows, :]
            low = pl.ds(pl.multiple_of(j * 256, 256), 256)
            high = pl.ds(pl.multiple_of(D + j * 256, 256), 256)
            lin = jnp.dot(
                left, in_full[:, :, :, :, low].reshape(D, 256), preferred_element_type=F32
            )
            gate = jnp.dot(
                left, in_full[:, :, :, :, high].reshape(D, 256), preferred_element_type=F32
            )
            gate = jax.nn.sigmoid(gate)
            linear[rows, low] = lin.astype(BF16)
            opened[rows, low] = gate.astype(BF16)
            gated = (lin * gate * valid(half * 256, 256)).astype(BF16).astype(F32)
            inside = pl.ds(16 + half * 256, 256)
            padded[2 * j, inside, :] = gated[:, :128]
            padded[2 * j + 1, inside, :] = gated[:, 128:]


def taps_sum(source, i, base, tap):
    total = None
    for r in range(8):
        window = source[i, pl.ds(base + r + 1, 152), :]
        for j in range(4):
            k = 8 * j + r
            if k < 31:
                term = tap(k) * window[8 * j : 8 * j + 128]
                total = term if total is None else total + term
    return total


def conv_stage(bases, padded, taps, temporal):
    @pl.loop(0, 12)
    def _(i):
        for base in bases:
            total = taps_sum(padded, i, base, lambda k: taps[k : k + 1, rows_of(i, 128)])
            temporal[pl.ds(base, 128), pl.ds(pl.multiple_of(i * 128, 128), 128)] = total


def mid_stage(temporal, gain, smooth_grad, smooth, grad_padded, mid_term):
    mid_term[...] = jnp.zeros_like(mid_term)

    @pl.loop(0, 16)
    def _(i):
        rows = rows_of(i, 32)
        value = temporal[rows, :]
        mean = jnp.mean(value, -1, keepdims=True)
        center = value - mean
        inverse = lax.rsqrt(jnp.mean(center * center, -1, keepdims=True) + EPS)
        hat = center * inverse
        scaled = hat * gain[...]
        s = jax.nn.sigmoid(scaled)
        smooth[rows, :] = swapped((scaled * s).astype(BF16))
        grad = smooth_grad[rows, :].astype(F32) * (s * (1.0 + scaled * (1.0 - s)))
        mid_term[...] += jnp.sum((grad * hat).reshape(4, 8, D), 0)
        q = grad * gain[...]
        result = inverse * (
            q - jnp.mean(q, -1, keepdims=True) - hat * jnp.mean(q * hat, -1, keepdims=True)
        )
        result = result.astype(BF16).astype(F32)
        inside = pl.ds(pl.multiple_of(16 + i * 32, 16), 32)
        for t in range(12):
            grad_padded[t, inside, :] = result[:, t * 128 : (t + 1) * 128]


def backward_conv(first, last, padded, grad_padded, taps, linear, opened, valid, hidden_grad, sums):
    @pl.loop(first, last)
    def _(i):
        columns = pl.ds(pl.multiple_of(i * 128, 128), 128)
        high = pl.ds(pl.multiple_of(D + i * 128, 128), 128)
        for base in range(0, 512, 128):
            rows = pl.ds(base, 128)
            grad = taps_sum(grad_padded, i, base, lambda k: taps[30 - k : 31 - k, columns])
            grad = grad * valid(base, 128)
            gate = opened[rows, columns].astype(F32)
            direct = grad * gate
            hidden_grad[rows, columns] = direct.astype(BF16)
            hidden_grad[rows, high] = (
                direct * linear[rows, columns].astype(F32) * (1.0 - gate)
            ).astype(BF16)
            here = grad_padded[i, pl.ds(base + 16, 128), :]
            for r in range(8):
                window = padded[i, pl.ds(base + r + 1, 152), :]
                for j in range(4):
                    k = 8 * j + r
                    if k < 31:
                        term = (window[8 * j : 8 * j + 128] * here).reshape(16, 8, 128)
                        term = jnp.sum(term, 0)
                        if base:
                            sums[i, k] += term
                        else:
                            sums[i, k] = term


def transposed_product(left, right):
    return lax.dot_general(
        left, right, (((1,), (1,)), ((), ())), preferred_element_type=F32
    )


def transpose_stage(source, own, other, c):
    for half, target in ((c, own), (1 - c, other)):

        @pl.loop(0, 6)
        def _(j):
            columns = pl.ds(pl.multiple_of(half * HALF + j * 128, 128), 128)
            for base in range(0, FRAMES, 128):
                block = source[pl.ds(base, 128), columns]
                target[rows_of(j, 128), pl.ds(base, 128)] = jnp.transpose(block)


def weight_grad(first, last, left, right, right_column, target, target_column):
    @pl.loop(first, last)
    def _(t):
        value = jnp.dot(
            left[...],
            right[:, pl.ds(pl.multiple_of(right_column(t), 256), 256)],
            preferred_element_type=F32,
        )
        target[:, :, :, pl.ds(pl.multiple_of(target_column(t), 256), 256)] = (
            value.astype(BF16).reshape(4, 4, ROWS, 256)
        )


def back_product(parts, left, full, result):
    for q in parts:
        yh, c = q // 2, q % 2
        weights = full[c, 2 * yh : 2 * yh + 2].reshape(384, full.shape[-1])
        result[:, q * 384 : (q + 1) * 384] = transposed_product(left[...], weights).astype(
            result.dtype
        )


def branch_stage(smooth, out_full, frames, valid, mixed):
    @pl.loop(0, 6)
    def _(j):
        columns = rows_of(j, 256)
        value = jnp.dot(
            smooth[...],
            out_full[:, :, :, :, columns].reshape(D, 256),
            preferred_element_type=F32,
        )
        mixed[:, columns] = (frames[:, columns].astype(F32) + valid(0, 512) * value).astype(BF16)


def frames_stage(frames, cotangent, gain, mean_ref, inverse_ref, normed_grad, result, in_term):
    in_term[...] = jnp.zeros_like(in_term)

    @pl.loop(0, 16)
    def _(i):
        rows = rows_of(i, 32)
        inverse = inverse_ref[rows, :]
        centred = (frames[rows, :].astype(F32) - mean_ref[rows, :]) * inverse
        grad = normed_grad[rows, :]
        in_term[...] += jnp.sum((grad * centred).reshape(4, 8, D), 0)
        p = grad * gain[...]
        change = inverse * (
            p - jnp.mean(p, -1, keepdims=True) - centred * jnp.mean(p * centred, -1, keepdims=True)
        )
        result[rows, :] = (cotangent[rows, :].astype(F32) + change).astype(BF16)


def edges(net, place, padded):
    tm = lax.axis_index("tm")
    rows = {"first": padded.at[:, 16:32, :], "last": padded.at[:, FRAMES : FRAMES + 16, :]}
    before, after = padded.at[:, 0:16, :], padded.at[:, FRAMES + 16 : FRAMES + 32, :]
    here = (lax.axis_index("utt"), lax.axis_index("wshard"))
    ahead = (here[0], around(tm, 1), here[1])
    behind = (here[0], around(tm, 3), here[1])
    slots = (net.send(rows["last"], before, ahead), net.send(rows["first"], after, behind))

    def arrive():
        net.wait(slots[0], before)
        net.wait(slots[1], after)
        padded[:, 0:16, :] = padded[:, 0:16, :] * (tm > 0).astype(F32)
        padded[:, FRAMES + 16 : FRAMES + 32, :] = padded[:, FRAMES + 16 : FRAMES + 32, :] * (
            tm < 3
        ).astype(F32)

    return arrive


def module_kernel(scale, tree, *refs):
    (
        length_ref, frames_hbm, cotangent_hbm, norm_gain_hbm, in_hbm, taps, mid_gain_hbm, out_hbm,
        mixed_hbm, grad_frames_hbm, grad_in, grad_out, grad_taps, grad_norm_hbm, grad_mid_hbm,
    ) = refs[:15]
    (
        in_full, out_full, frames, branch_grad, normed, smooth, linear, opened, padded, grad_padded,
        temporal, smooth_grad, hidden_grad, normed_t, smooth_t, other_t, mean_ref, inverse_ref,
        sums, mid_term, in_term, first_terms, second_terms, small, small_sum,
        norm_gain, mid_gain, grad_norm_gain, grad_mid_gain, sent, landed, local, bufs,
    ) = jax.tree_util.tree_unflatten(tree, refs[15:])
    place = Place()
    net = Net(place, sent, landed)
    c = place.c
    sibling = place.sibling()
    length = length_ref[0]
    start = lax.axis_index("tm") * FRAMES

    def valid(first, rows):
        return valid_rows(length, start, first, rows)

    loads = [
        pltpu.make_async_copy(in_hbm, in_full.at[c, place.y, place.z], local.at[0]),
        pltpu.make_async_copy(frames_hbm, frames, local.at[1]),
        pltpu.make_async_copy(cotangent_hbm, branch_grad.at[0:FRAMES], local.at[2]),
        pltpu.make_async_copy(out_hbm, out_full.at[c, place.y, place.z], local.at[3]),
        pltpu.make_async_copy(norm_gain_hbm, norm_gain.at[0], local.at[4]),
        pltpu.make_async_copy(mid_gain_hbm, mid_gain.at[0], local.at[5]),
    ]
    for load in loads:
        load.start()
    place.greet()
    gather_in, gather_out = Gather(net, place, in_full), Gather(net, place, out_full)
    loads[0].wait()
    gather_in.begin()
    loads[1].wait()
    loads[4].wait()
    loads[5].wait()
    norm = (frames, norm_gain, normed, mean_ref, inverse_ref)
    norm_stage(0, 6, *norm)
    gather_in.second()
    norm_stage(6, 16, *norm)
    gather_in.third()
    loads[2].wait()

    @pl.loop(0, 8)
    def _(i):
        rows = rows_of(i, 64)
        branch_grad[rows, :] = (branch_grad[rows, :].astype(F32) * valid(i * 64, 64)).astype(BF16)

    pair_branch = net.send(branch_grad.at[0:FRAMES], branch_grad.at[FRAMES : 2 * FRAMES], sibling)
    transpose_stage(normed, normed_t.at[:, 0:FRAMES], other_t, c)
    pair_normed = net.send(other_t, normed_t.at[:, FRAMES : 2 * FRAMES], sibling)
    gather_in.fourth()
    loads[3].wait()
    out_first = net.count
    gather_out.begin()
    gather_in.finish()
    gather_out.second()
    hidden = (normed, in_full, linear, opened, padded, valid)
    hidden_stage(0, 3, *hidden)
    gather_out.third()
    hidden_stage(3, 6, *hidden)
    arrive = edges(net, place, padded)
    gather_out.fourth()
    conv_stage((128, 256), padded, taps, temporal)
    arrive()
    conv_stage((0, 384), padded, taps, temporal)
    gather_out.finish()
    out_last = net.count
    back_product(range(4), branch_grad.at[0:FRAMES], out_full, smooth_grad)
    mid_stage(temporal, mid_gain, smooth_grad, smooth, grad_padded, mid_term)
    arrive = edges(net, place, grad_padded)

    net.gone([pair_normed])
    transpose_stage(smooth, smooth_t.at[:, 0:FRAMES], other_t, c)
    pair_smooth = net.send(other_t, smooth_t.at[:, FRAMES : 2 * FRAMES], sibling)
    branch_stage(smooth, out_full, frames, valid, normed)
    store_mixed = pltpu.make_async_copy(normed, mixed_hbm, local.at[0])
    store_mixed.start()
    net.wait(pair_branch, branch_grad.at[FRAMES : 2 * FRAMES])
    net.wait(pair_smooth, smooth_t.at[:, FRAMES : 2 * FRAMES])
    weight_grad(0, 6, smooth_t, branch_grad, lambda t: t * 256, first_terms, lambda t: t * 256)
    scatter_out = Scatter(net, place, first_terms, bufs[0])
    scatter_out.step_far()
    arrive()
    conv = (padded, grad_padded, taps, linear, opened, valid, hidden_grad, sums)
    pair_hidden = []

    def backward(group):
        backward_conv(2 * group, 2 * group + 2, *conv)
        for column in (256 * group, D + 256 * group):
            own = hidden_grad.at[0:FRAMES, column : column + 256]
            there = hidden_grad.at[FRAMES : 2 * FRAMES, column : column + 256]
            pair_hidden.append((net.send(own, there, sibling), there))

    def hidden_arrive(groups):
        for _ in range(2 * groups):
            net.wait(*pair_hidden.pop(0))

    def grad_half(first, last, half, target):
        weight_grad(
            first,
            last,
            normed_t,
            hidden_grad,
            lambda t: lax.rem(t, 2) * D + half * HALF + lax.div(t, 2) * 256,
            target,
            lambda t: lax.rem(t, 2) * HALF + lax.div(t, 2) * 256,
        )

    third_terms = out_full.at[0]
    scatter_one = Scatter(net, place, second_terms, bufs[1])
    scatter_two = Scatter(net, place, third_terms, bufs[2])
    backward(0)
    backward(1)
    backward(2)
    scatter_out.step_near()
    net.wait(pair_normed, normed_t.at[:, FRAMES : 2 * FRAMES])
    hidden_arrive(3)
    grad_half(0, 6, 0, second_terms)
    scatter_one.step_far()
    backward(3)
    backward(4)
    scatter_one.step_near()
    scatter_out.step_second()
    backward(5)
    net.gone(range(out_first, out_last))
    hidden_arrive(2)
    grad_half(0, 4, 1, third_terms)
    hidden_arrive(1)
    grad_half(4, 6, 1, third_terms)
    scatter_two.step_far()
    scatter_out.step_third()
    scatter_one.step_second()
    reload = pltpu.make_async_copy(cotangent_hbm, opened, local.at[1])
    reload.start()

    def store_out(column, value):
        grad_out[:, column : column + 128] = value * scale

    def store_in(half):
        def store(column, value):
            to = half * HALF + column + (HALF if column >= HALF else 0)
            grad_in[:, to : to + 128] = value * scale

        return store

    own_hidden = hidden_grad.at[0:FRAMES]
    back_product((0, 1), own_hidden, in_full, temporal)
    scatter_two.step_near()
    back_product((2,), own_hidden, in_full, temporal)
    scatter_out.step_spread()
    scatter_one.step_third()
    back_product((3,), own_hidden, in_full, temporal)
    reload.wait()
    frames_stage(
        frames, opened, norm_gain, mean_ref, inverse_ref, temporal, smooth, in_term
    )
    store_frames = pltpu.make_async_copy(smooth, grad_frames_hbm, local.at[2])
    store_frames.start()
    for i in range(12):
        lanes = slice((i % 2) * 128, (i % 2) * 128 + 128)
        columns = slice(i * 128, i * 128 + 128)
        core, portion = (i // 2) % 2, i // 4
        small[core, portion, 0:31, lanes] = jnp.sum(sums[i], 1)[0:31]
        small[core, portion, 31:32, lanes] = jnp.sum(in_term[:, columns], 0, keepdims=True)
        small[core, portion, 32:33, lanes] = jnp.sum(mid_term[:, columns], 0, keepdims=True)
        small[core, portion, 33:40, lanes] = jnp.zeros((7, 128), F32)
    total = Total(net, place, small, *bufs[3], small_sum)
    total.to_sibling()
    scatter_two.step_second()
    total.begin()
    scatter_one.step_spread()
    scatter_out.step_last(store_out)
    scatter_two.step_third()
    total.step(1)
    scatter_one.step_last(store_in(0))
    scatter_two.step_spread()
    total.step(2)
    total.spread()
    scatter_two.step_last(store_in(1))
    total.last()
    for core in range(2):
        for portion in range(3):
            columns = slice(portion * 512 + core * 256, portion * 512 + core * 256 + 256)
            grad_taps[:, columns] = small_sum[core, portion, 0:31, :] * scale
            grad_norm_gain[:, columns] = small_sum[core, portion, 31:32, :] * scale
            grad_mid_gain[:, columns] = small_sum[core, portion, 32:33, :] * scale
    stores = [
        pltpu.make_async_copy(grad_norm_gain.at[0], grad_norm_hbm, local.at[4]),
        pltpu.make_async_copy(grad_mid_gain.at[0], grad_mid_hbm, local.at[5]),
    ]
    for store in stores:
        store.start()
    store_mixed.wait()
    store_frames.wait()
    for store in stores:
        store.wait()
    net.drain()


def settle_kernel(*refs):
    count = (len(refs) - 1) // 2
    copies = [
        pltpu.make_async_copy(src, dst, refs[-1].at[i])
        for i, (src, dst) in enumerate(zip(refs[:count], refs[count:-1]))
    ]
    for copy in copies:
        copy.start()
    for copy in copies:
        copy.wait()


def settle(*arrays):
    arrays = [a[None] if i < 2 else a for i, a in enumerate(arrays)]
    inside = pl.BlockSpec(memory_space=pltpu.VMEM)
    outside = pl.BlockSpec(memory_space=pltpu.HBM)
    return tuple(
        pl.pallas_call(
            settle_kernel,
            out_shape=[jax.ShapeDtypeStruct(a.shape, a.dtype) for a in arrays],
            in_specs=[inside] * len(arrays),
            out_specs=[outside] * len(arrays),
            scratch_shapes=[pltpu.SemaphoreType.DMA((len(arrays),))],
        )(*arrays)
    )


def body(frames, lengths, cotangent, norm_gain, w_in, kernel, mid_gain, w_out):
    scale = 1.0 / math.sqrt(
        FRAMES * lax.axis_size("utt") * lax.axis_size("tm") * lax.axis_size("wshard")
    )
    block = (FRAMES, D)
    copies = 2 * GATHER_COPIES + 3 * SCATTER_COPIES + TOTAL_COPIES + 32
    scratch = [
        pltpu.VMEM((2, 4, 4, ROWS, 2 * D), BF16),
        pltpu.VMEM((2, 4, 4, ROWS, D), BF16),
        pltpu.VMEM(block, BF16),
        pltpu.VMEM((2 * FRAMES, D), BF16),
        pltpu.VMEM(block, BF16),
        pltpu.VMEM(block, BF16),
        pltpu.VMEM(block, BF16),
        pltpu.VMEM(block, BF16),
        pltpu.VMEM((12, FRAMES + 32, 128), F32),
        pltpu.VMEM((12, FRAMES + 32, 128), F32),
        pltpu.VMEM(block, F32),
        pltpu.VMEM(block, BF16),
        pltpu.VMEM((2 * FRAMES, 2 * D), BF16),
        pltpu.VMEM((HALF, 2 * FRAMES), BF16),
        pltpu.VMEM((HALF, 2 * FRAMES), BF16),
        pltpu.VMEM((HALF, FRAMES), BF16),
        pltpu.VMEM((FRAMES, 1), F32),
        pltpu.VMEM((FRAMES, 1), F32),
        pltpu.VMEM((12, 32, 8, 128), F32),
        pltpu.VMEM((8, D), F32),
        pltpu.VMEM((8, D), F32),
        pltpu.VMEM((4, 4, ROWS, D), BF16),
        pltpu.VMEM((4, 4, ROWS, D), BF16),
        pltpu.VMEM((2, 3, 40, 256), F32),
        pltpu.VMEM((2, 3, 40, 256), F32),
        pltpu.VMEM((1, D), F32),
        pltpu.VMEM((1, D), F32),
        pltpu.VMEM((1, D), F32),
        pltpu.VMEM((1, D), F32),
        pltpu.SemaphoreType.DMA((copies,)),
        pltpu.SemaphoreType.DMA((copies,)),
        pltpu.SemaphoreType.DMA((6,)),
        [Scatter.scratch(D), Scatter.scratch(D), Scatter.scratch(D), Total.scratch(40, 256)],
    ]
    leaves, tree = jax.tree_util.tree_flatten(scratch)
    anywhere = pl.BlockSpec(memory_space=pl.ANY)
    inside = pl.BlockSpec(memory_space=pltpu.VMEM)
    scalar = pl.BlockSpec(memory_space=pltpu.SMEM)
    outs = pl.pallas_call(
        functools.partial(module_kernel, scale, tree),
        out_shape=[
            jax.ShapeDtypeStruct(block, BF16),
            jax.ShapeDtypeStruct(block, BF16),
            jax.ShapeDtypeStruct((ROWS, 2 * D), F32),
            jax.ShapeDtypeStruct((ROWS, D), F32),
            jax.ShapeDtypeStruct((31, D), F32),
            jax.ShapeDtypeStruct((D,), F32),
            jax.ShapeDtypeStruct((D,), F32),
        ],
        in_specs=[scalar, anywhere, anywhere, anywhere, anywhere, inside, anywhere, anywhere],
        out_specs=[anywhere, anywhere, inside, inside, inside, anywhere, anywhere],
        scratch_shapes=leaves,
        compiler_params=pltpu.CompilerParams(
            collective_id=0, has_side_effects=True, vmem_limit_bytes=63 * 2**20
        ),
    )(
        lengths, frames[0], cotangent[0], norm_gain, w_in, kernel, mid_gain, w_out
    )
    return settle(*outs)


def solution(mesh):
    return jax.shard_map(
        body,
        mesh=mesh,
        in_specs=(
            P(("utt", "wshard"), "tm", None),
            P(("utt", "wshard")),
            P(("utt", "wshard"), "tm", None),
            P(),
            P(("tm", "wshard"), None),
            P(),
            P(),
            P(("tm", "wshard"), None),
        ),
        out_specs=(
            P(("utt", "wshard"), "tm", None),
            P(("utt", "wshard"), "tm", None),
            P(("tm", "wshard"), None),
            P(("tm", "wshard"), None),
            P(),
            P(),
            P(),
        ),
        check_vma=False,
    )
```

```python
import functools
import math

import jax
import jax.numpy as jnp
from jax import lax
from jax.experimental import pallas as pl
from jax.experimental.pallas import tpu as pltpu
from jax.sharding import PartitionSpec as P

EPS = 1e-05
MESH = pl.DeviceIdType.MESH
F32 = jnp.float32
BF16 = jnp.bfloat16
ROWS = 48
D = 1536
FRAMES = 512
HALF = D // 2


def around(value, shift):
    return lax.rem(value + shift, 4)


class Place:
    def __init__(self):
        tm, ws = lax.axis_index("tm"), lax.axis_index("wshard")
        self.x = lax.axis_index("utt")
        self.c = lax.rem(tm, 2)
        self.y = lax.div(tm, 2) * 2 + lax.div(ws, 4)
        self.z = lax.rem(ws, 4)

    def device(self, x, y, z, c):
        return (x, lax.div(y, 2) * 2 + c, lax.rem(y, 2) * 4 + z)

    def at(self, axis, shift):
        x, y, z = self.x, self.y, self.z
        if axis == "x":
            x = around(x, shift)
        if axis == "y":
            y = around(y, shift)
        if axis == "z":
            z = around(z, shift)
        return self.device(x, y, z, self.c)

    def sibling(self):
        return self.device(self.x, self.y, self.z, 1 - self.c)

    def greet(self):
        barrier = pltpu.get_barrier_semaphore()
        others = [self.at(axis, shift) for axis in "xyz" for shift in (1, 2, 3)]
        others.append(self.sibling())
        others.append(self.device(self.x, around(self.y, 2), self.z, 1 - self.c))
        for other in others:
            pl.semaphore_signal(barrier, inc=1, device_id=other, device_id_type=MESH)
        pl.semaphore_wait(barrier, len(others))


class Net:
    def __init__(self, place, sent, landed):
        self.place, self.sent, self.landed = place, sent, landed
        self.count = 0
        self.flying = {}

    def send(self, src, dst, device):
        slot = self.count
        self.count += 1
        copy = pltpu.make_async_remote_copy(
            src_ref=src,
            dst_ref=dst,
            send_sem=self.sent.at[slot],
            recv_sem=self.landed.at[slot],
            device_id=device,
            device_id_type=MESH,
        )
        copy.start()
        self.flying[slot] = copy
        return slot

    def wait(self, slot, dst):
        pltpu.make_async_remote_copy(
            src_ref=dst,
            dst_ref=dst,
            send_sem=self.sent.at[slot],
            recv_sem=self.landed.at[slot],
            device_id=self.place.sibling(),
            device_id_type=MESH,
        ).wait_recv()

    def gone(self, slots):
        for slot in slots:
            if slot in self.flying:
                self.flying.pop(slot).wait_send()

    def drain(self):
        self.gone(list(self.flying))


class Gather:
    def __init__(self, net, place, full):
        self.net, self.place, self.full = net, place, full
        self.portion = full.shape[-1] // 3
        self.quarter = self.portion // 4

    def part_a(self, dy, dz):
        p = self.place
        y = around(p.y, 4 - dy)
        z = around(p.z, 4 - dz)
        return self.full.at[p.c, y, z, :, pl.ds(0, self.portion)]

    def part_b(self, dy, dz):
        p = self.place
        y = around(p.y, 4 - dy)
        z = around(p.z, 4 - dz)
        return self.full.at[p.c, y, z, :, pl.ds(self.portion, self.portion)]

    def columns(self, which, dx):
        x = around(self.place.x, 4 - dx)
        start = pl.multiple_of(which * self.portion + x * self.quarter, 128)
        return pl.ds(start, self.quarter)

    def quarter_b(self, dy, dx):
        p = self.place
        return self.full.at[p.c, around(p.y, 4 - dy), p.z, :, self.columns(1, dx)]

    def quarter_c(self, dy, dz, dx):
        p = self.place
        return self.full.at[
            p.c, around(p.y, 4 - dy), around(p.z, 4 - dz), :, self.columns(2, dx)
        ]

    def group_c(self, group, dx):
        p = self.place
        dy, dz = group
        if dz is None:
            return self.full.at[p.c, around(p.y, 4 - dy), :, :, self.columns(2, dx)]
        return self.quarter_c(dy, dz, dx)

    def share(self, name, c):
        p = self.place
        kind, shift = name
        if kind == "a":
            return self.full.at[c, around(p.y, 4 - shift), :, :, pl.ds(0, self.portion)]
        if kind == "b":
            return self.full.at[
                c, :, around(p.z, 4 - shift), :, pl.ds(self.portion, self.portion)
            ]
        return self.full.at[c, :, :, :, self.columns(2, shift)]

    def give(self, name):
        ref = self.share(name, self.place.c)
        self.shared.append((name, self.net.send(ref, ref, self.place.sibling())))

    def begin(self):
        net, p = self.net, self.place
        self.shared = []
        own_b, own_c = self.quarter_b(0, 0), self.quarter_c(0, 0, 0)
        own_a, own_whole_b = self.part_a(0, 0), self.part_b(0, 0)
        self.c_z, self.b_y, self.a_z = {}, {}, {}
        self.c_y, self.a_y, self.b_z = {}, {}, {}
        self.c_x, self.b_x = {}, {}
        for shift in (1, 3, 2):
            self.c_z[shift] = net.send(own_c, own_c, p.at("z", shift))
            self.b_y[shift] = net.send(own_b, own_b, p.at("y", shift))
        for shift in (1, 3, 2):
            self.a_z[shift] = net.send(own_a, own_a, p.at("z", shift))
            self.c_y[shift, 0] = net.send(own_c, own_c, p.at("y", shift))
        for shift in (1, 3):
            self.a_y[shift, 0] = net.send(own_a, own_a, p.at("y", shift))
            self.b_z[shift, 0] = net.send(own_whole_b, own_whole_b, p.at("z", shift))

    def second(self):
        net, p = self.net, self.place
        for d in (1, 3, 2):
            ref = self.quarter_c(0, d, 0)
            net.wait(self.c_z[d], ref)
            for shift in (1, 3, 2):
                self.c_y[shift, d] = net.send(ref, ref, p.at("y", shift))
            for shift in (1, 3):
                self.c_x[shift, (0, d)] = net.send(ref, ref, p.at("x", shift))
            ref = self.quarter_b(d, 0)
            net.wait(self.b_y[d], ref)
            for shift in (1, 3, 2):
                self.b_x[shift, d] = net.send(ref, ref, p.at("x", shift))
        for d in (1, 3, 2):
            ref = self.part_a(0, d)
            net.wait(self.a_z[d], ref)
            for shift in (1, 3):
                self.a_y[shift, d] = net.send(ref, ref, p.at("y", shift))
        self.give(("a", 0))

    def third(self):
        net, p = self.net, self.place
        for d in (1, 3, 2):
            for shift in (1, 3, 2):
                net.wait(self.b_x[shift, d], self.quarter_b(d, shift))
            ref = self.part_b(d, 0)
            for shift in (1, 3):
                self.b_z[shift, d] = net.send(ref, ref, p.at("z", shift))
            for dz in range(4):
                net.wait(self.c_y[d, dz], self.quarter_c(d, dz, 0))
            ref = self.group_c((d, None), 0)
            for shift in (1, 3):
                self.c_x[shift, (d, None)] = net.send(ref, ref, p.at("x", shift))
        self.give(("b", 0))
        self.give(("c", 0))

    def onward(self, table, keys, region, axis):
        net, p = self.net, self.place
        far = {}
        for number, key in enumerate(keys):
            for shift in (1, 3):
                ref = region(key, shift)
                net.wait(table[shift, key], ref)
                if (number % 2 == 0) == (shift == 1):
                    far[key] = net.send(ref, ref, p.at(axis, shift))
        return far

    def fourth(self):
        groups = [(0, 1), (0, 3), (0, 2), (1, None), (3, None), (2, None)]
        self.groups = groups
        self.a_far = self.onward(self.a_y, (0, 1, 3, 2), lambda d, s: self.part_a(s, d), "y")
        self.b_far = self.onward(self.b_z, (0, 1, 3, 2), lambda d, s: self.part_b(d, s), "z")
        self.c_far = self.onward(self.c_x, groups, lambda g, s: self.group_c(g, s), "x")
        for shift in (1, 3):
            for kind in "abc":
                self.give((kind, shift))

    def finish(self):
        net, p = self.net, self.place
        for d in (0, 1, 3, 2):
            net.wait(self.a_far[d], self.part_a(2, d))
        self.give(("a", 2))
        for d in (0, 1, 3, 2):
            net.wait(self.b_far[d], self.part_b(d, 2))
        self.give(("b", 2))
        for group in self.groups:
            net.wait(self.c_far[group], self.group_c(group, 2))
        self.give(("c", 2))
        for name, slot in self.shared:
            net.wait(slot, self.share(name, 1 - p.c))


GATHER_COPIES = 90


def add_into(target, term):
    target[...] = (target[...].astype(F32) + term[...].astype(F32)).astype(target.dtype)


class Scatter:
    def __init__(self, net, place, terms, bufs):
        self.net, self.place, self.terms = net, place, terms
        self.portion = terms.shape[-1] // 3
        self.quarter = self.portion // 4
        self.near, self.mid, self.final, self.done = bufs
        self.slots = {}

    @staticmethod
    def scratch(columns):
        portion, quarter = columns // 3, columns // 12
        return [
            [
                pltpu.VMEM((2, 2, ROWS, portion), BF16),
                pltpu.VMEM((2, 2, ROWS, portion), BF16),
                pltpu.VMEM((2, 2, 4, ROWS, quarter), BF16),
                pltpu.VMEM((2, 4, ROWS, portion), BF16),
                pltpu.VMEM((2, 4, ROWS, portion), BF16),
                pltpu.VMEM((2, 4, 4, ROWS, quarter), BF16),
            ],
            [
                pltpu.VMEM((3, ROWS, portion), BF16),
                pltpu.VMEM((3, 4, ROWS, quarter), BF16),
                pltpu.VMEM((3, 4, ROWS, quarter), BF16),
            ],
            [pltpu.VMEM((3, ROWS, quarter), BF16)] * 3,
            pltpu.VMEM((4, 3, ROWS, quarter), BF16),
        ]

    def columns(self, which, x):
        start = pl.multiple_of(which * self.portion + x * self.quarter, 128)
        return pl.ds(start, self.quarter)

    def whole(self, which):
        return pl.ds(which * self.portion, self.portion)

    def first(self, which, shift, half=None):
        p, of = self.place, self.terms
        part = slice(None) if half is None else pl.ds(2 * half, 2)
        if which == 0:
            return of.at[around(p.y, shift), part, :, self.whole(0)]
        if which == 1:
            return of.at[part, around(p.z, shift), :, self.whole(1)]
        return of.at[part, :, :, self.columns(2, around(p.x, shift))]

    def second(self, which, shift):
        p, mine = self.place, self.terms
        if which == 0:
            return mine.at[p.y, around(p.z, shift), :, self.whole(0)]
        if which == 1:
            return mine.at[:, p.z, :, self.columns(1, around(p.x, shift))]
        return mine.at[around(p.y, shift), :, :, self.columns(2, p.x)]

    def third(self, which, shift):
        p, mine = self.place, self.terms
        if which == 0:
            return mine.at[p.y, p.z, :, self.columns(0, around(p.x, shift))]
        if which == 1:
            return mine.at[around(p.y, shift), p.z, :, self.columns(1, p.x)]
        return mine.at[p.y, around(p.z, shift), :, self.columns(2, p.x)]

    AXES = (("y", "z", "x"), ("z", "x", "y"), ("x", "y", "z"))

    def step_far(self):
        net, p = self.net, self.place
        for which in range(3):
            axis = self.AXES[which][0]
            for half, shift in ((0, 1), (1, 3)):
                self.slots["far", which, half] = net.send(
                    self.first(which, 2, half),
                    self.near[which].at[half],
                    p.at(axis, shift),
                )

        for which in range(3):
            axis = self.AXES[which][0]
            for half, shift in ((0, 1), (1, 3)):
                self.slots["free", which, half] = net.send(
                    self.first(which, shift, 1 - half),
                    self.near[3 + which].at[half, pl.ds(2 - 2 * half, 2)],
                    p.at(axis, shift),
                )

    def step_near(self):
        net, p = self.net, self.place
        for which in range(3):
            axis = self.AXES[which][0]
            for half, shift in ((0, 1), (1, 3)):
                came = self.near[which].at[half]
                net.wait(self.slots["far", which, half], came)
                target = self.first(which, shift, half)
                for i in range(2):
                    add_into(target.at[i], came.at[i])
                self.slots["near", which, half] = net.send(
                    self.first(which, shift, half),
                    self.near[3 + which].at[half, pl.ds(2 * half, 2)],
                    p.at(axis, shift),
                )

    def step_second(self):
        net, p = self.net, self.place
        for which in range(3):
            axis = self.AXES[which][1]
            target = self.first(which, 0)
            for half in range(2):
                came = self.near[3 + which].at[half]
                net.wait(self.slots["free", which, half], came.at[pl.ds(2 - 2 * half, 2)])
                net.wait(self.slots["near", which, half], came.at[pl.ds(2 * half, 2)])
                for i in range(4):
                    add_into(target.at[i], came.at[i])
            for shift in (2, 1, 3):
                self.slots["second", which, shift] = net.send(
                    self.second(which, shift), self.mid[which].at[shift - 1], p.at(axis, shift)
                )

    def step_third(self):
        net, p = self.net, self.place
        for which in range(3):
            axis = self.AXES[which][2]
            target = self.second(which, 0)
            for shift in (1, 3, 2):
                came = self.mid[which].at[shift - 1]
                net.wait(self.slots["second", which, shift], came)
                if which == 0:
                    add_into(target, came)
                else:
                    for i in range(4):
                        add_into(target.at[i], came.at[i])
            for shift in (2, 1, 3):
                self.slots["third", which, shift] = net.send(
                    self.third(which, shift), self.final[which].at[shift - 1], p.at(axis, shift)
                )

    def step_spread(self):
        net, p = self.net, self.place
        for which in range(3):
            total = self.third(which, 0)[...].astype(F32)
            for shift in (1, 3, 2):
                came = self.final[which].at[shift - 1]
                net.wait(self.slots["third", which, shift], came)
                total = total + came[...].astype(F32)
            self.done[p.x, which] = total.astype(BF16)
        for shift in (2, 1, 3):
            self.slots["spread", shift] = net.send(
                self.done.at[p.x], self.done.at[p.x], p.at("x", shift)
            )

    def step_last(self, store):
        net, p = self.net, self.place
        for shift in (1, 3, 2):
            net.wait(self.slots["spread", shift], self.done.at[around(p.x, 4 - shift)])
        for which in range(3):
            for x in range(4):
                store(which * self.portion + x * self.quarter, self.done[x, which].astype(F32))


SCATTER_COPIES = 39


class Total:
    ORDERS = ("xyz", "yzx", "zxy")

    def __init__(self, net, place, terms, pair, stages, out):
        self.net, self.place, self.terms, self.pairbuf = net, place, terms, pair
        self.stages, self.out = stages, out
        self.slots = {}

    @staticmethod
    def scratch(rows, width):
        return [
            pltpu.VMEM((3, rows, width), F32),
            pltpu.VMEM((3, 3, 4, rows, width), F32),
        ]

    def coordinate(self, axis):
        return {"x": self.place.x, "y": self.place.y, "z": self.place.z}[axis]

    def to_sibling(self):
        p = self.place
        self.slots["pair"] = self.net.send(self.terms.at[1 - p.c], self.pairbuf, p.sibling())

    def put(self, stage, portion, value):
        axis = self.ORDERS[portion][stage]
        own = self.stages.at[stage, portion, self.coordinate(axis)]
        own[...] = value
        for shift in (2, 1, 3):
            self.slots[stage, portion, shift] = self.net.send(own, own, self.place.at(axis, shift))

    def begin(self):
        self.net.wait(self.slots["pair"], self.pairbuf)
        for portion in range(3):
            self.put(0, portion, self.terms[self.place.c, portion] + self.pairbuf[portion])

    def collect(self, stage, portion):
        axis = self.ORDERS[portion][stage]
        for shift in (1, 3, 2):
            other = around(self.coordinate(axis), 4 - shift)
            self.net.wait(self.slots[stage, portion, shift], self.stages.at[stage, portion, other])
        s = self.stages
        return (s[stage, portion, 0] + s[stage, portion, 1]) + (
            s[stage, portion, 2] + s[stage, portion, 3]
        )

    def step(self, stage):
        for portion in range(3):
            self.put(stage, portion, self.collect(stage - 1, portion))

    def spread(self):
        p = self.place
        for portion in range(3):
            self.out[p.c, portion] = self.collect(2, portion)
        self.slots["back"] = self.net.send(self.out.at[p.c], self.out.at[p.c], p.sibling())

    def last(self):
        self.net.wait(self.slots["back"], self.out.at[1 - self.place.c])


TOTAL_COPIES = 32


def swapped(value):
    return jnp.concatenate(
        [value[:, :384], value[:, 768:1152], value[:, 384:768], value[:, 1152:]], axis=1
    )


def rows_of(i, size):
    return pl.ds(pl.multiple_of(i * size, size), size)


def valid_rows(length, first, start, rows):
    position = first + start + lax.broadcasted_iota(jnp.int32, (rows, 1), 0)
    return (position < length).astype(F32)


def norm_stage(first, last, frames, gain, normed, mean_ref, inverse_ref):
    @pl.loop(first, last)
    def _(i):
        rows = rows_of(i, 32)
        value = frames[rows, :].astype(F32)
        mean = jnp.mean(value, -1, keepdims=True)
        center = value - mean
        inverse = lax.rsqrt(jnp.mean(center * center, -1, keepdims=True) + EPS)
        mean_ref[rows, :] = mean
        inverse_ref[rows, :] = inverse
        normed[rows, :] = swapped((center * inverse * gain[...]).astype(BF16))


def hidden_stage(first, last, normed, in_full, linear, opened, padded, valid):
    @pl.loop(first, last)
    def _(j):
        for half in range(2):
            rows = pl.ds(half * 256, 256)
            left = normed[rows, :]
            low = pl.ds(pl.multiple_of(j * 256, 256), 256)
            high = pl.ds(pl.multiple_of(D + j * 256, 256), 256)
            lin = jnp.dot(
                left, in_full[:, :, :, :, low].reshape(D, 256), preferred_element_type=F32
            )
            gate = jnp.dot(
                left, in_full[:, :, :, :, high].reshape(D, 256), preferred_element_type=F32
            )
            gate = jax.nn.sigmoid(gate)
            linear[rows, low] = lin.astype(BF16)
            opened[rows, low] = gate.astype(BF16)
            gated = (lin * gate * valid(half * 256, 256)).astype(BF16).astype(F32)
            inside = pl.ds(16 + half * 256, 256)
            padded[2 * j, inside, :] = gated[:, :128]
            padded[2 * j + 1, inside, :] = gated[:, 128:]


def taps_sum(source, i, base, tap):
    total = None
    for r in range(8):
        window = source[i, pl.ds(base + r + 1, 152), :]
        for j in range(4):
            k = 8 * j + r
            if k < 31:
                term = tap(k) * window[8 * j : 8 * j + 128]
                total = term if total is None else total + term
    return total


def conv_stage(bases, padded, taps, temporal):
    @pl.loop(0, 12)
    def _(i):
        for base in bases:
            total = taps_sum(padded, i, base, lambda k: taps[k : k + 1, rows_of(i, 128)])
            temporal[pl.ds(base, 128), pl.ds(pl.multiple_of(i * 128, 128), 128)] = total


def mid_stage(temporal, gain, smooth_grad, smooth, grad_padded, mid_term):
    mid_term[...] = jnp.zeros_like(mid_term)

    @pl.loop(0, 16)
    def _(i):
        rows = rows_of(i, 32)
        value = temporal[rows, :]
        mean = jnp.mean(value, -1, keepdims=True)
        center = value - mean
        inverse = lax.rsqrt(jnp.mean(center * center, -1, keepdims=True) + EPS)
        hat = center * inverse
        scaled = hat * gain[...]
        s = jax.nn.sigmoid(scaled)
        smooth[rows, :] = swapped((scaled * s).astype(BF16))
        grad = swapped(smooth_grad[rows, :].astype(F32)) * (s * (1.0 + scaled * (1.0 - s)))
        mid_term[...] += jnp.sum((grad * hat).reshape(4, 8, D), 0)
        q = grad * gain[...]
        result = inverse * (
            q - jnp.mean(q, -1, keepdims=True) - hat * jnp.mean(q * hat, -1, keepdims=True)
        )
        result = result.astype(BF16).astype(F32)
        inside = pl.ds(pl.multiple_of(16 + i * 32, 16), 32)
        for t in range(12):
            grad_padded[t, inside, :] = result[:, t * 128 : (t + 1) * 128]


def backward_conv(first, last, padded, grad_padded, taps, linear, opened, valid, hidden_grad, sums):
    @pl.loop(first, last)
    def _(i):
        columns = pl.ds(pl.multiple_of(i * 128, 128), 128)
        high = pl.ds(pl.multiple_of(D + i * 128, 128), 128)
        for base in range(0, 512, 128):
            rows = pl.ds(base, 128)
            grad = taps_sum(grad_padded, i, base, lambda k: taps[30 - k : 31 - k, columns])
            grad = grad * valid(base, 128)
            gate = opened[rows, columns].astype(F32)
            direct = grad * gate
            hidden_grad[rows, columns] = direct.astype(BF16)
            hidden_grad[rows, high] = (
                direct * linear[rows, columns].astype(F32) * (1.0 - gate)
            ).astype(BF16)
            here = grad_padded[i, pl.ds(base + 16, 128), :]
            for r in range(8):
                window = padded[i, pl.ds(base + r + 1, 152), :]
                for j in range(4):
                    k = 8 * j + r
                    if k < 31:
                        term = (window[8 * j : 8 * j + 128] * here).reshape(16, 8, 128)
                        term = jnp.sum(term, 0)
                        if base:
                            sums[i, k] += term
                        else:
                            sums[i, k] = term


def transposed_product(left, right):
    return lax.dot_general(
        left, right, (((1,), (1,)), ((), ())), preferred_element_type=F32
    )


def transpose_stage(source, own, other, c):
    for half, target in ((c, own), (1 - c, other)):

        @pl.loop(0, 6)
        def _(j):
            columns = pl.ds(pl.multiple_of(half * HALF + j * 128, 128), 128)
            for base in range(0, FRAMES, 128):
                block = source[pl.ds(base, 128), columns]
                target[rows_of(j, 128), pl.ds(base, 128)] = jnp.transpose(block)


def weight_grad(left, right, right_column, target):
    @pl.loop(0, 2)
    def _(t):
        columns = pl.ds(pl.multiple_of(right_column(t), 256), HALF)
        for y in range(4):
            value = jnp.dot(
                left[y * 192 : y * 192 + 192, :],
                right[:, columns],
                preferred_element_type=F32,
            )
            target[y, :, :, rows_of(t, HALF)] = value.astype(BF16).reshape(4, ROWS, HALF)


def back_product(c, left, full, result):
    for y in (0, 2):
        weights = full[c, y : y + 2].reshape(384, full.shape[-1])
        columns = pl.ds(c * HALF + y * 192, 384)
        result[:, columns] = transposed_product(left[...], weights).astype(result.dtype)


def branch_stage(smooth, out_full, frames, valid, mixed):
    @pl.loop(0, 6)
    def _(j):
        columns = rows_of(j, 256)
        value = jnp.dot(
            smooth[...],
            out_full[:, :, :, :, columns].reshape(D, 256),
            preferred_element_type=F32,
        )
        mixed[:, columns] = (frames[:, columns].astype(F32) + valid(0, 512) * value).astype(BF16)


def frames_stage(frames, cotangent, gain, mean_ref, inverse_ref, normed_grad, result, in_term):
    in_term[...] = jnp.zeros_like(in_term)

    @pl.loop(0, 16)
    def _(i):
        rows = rows_of(i, 32)
        inverse = inverse_ref[rows, :]
        centred = (frames[rows, :].astype(F32) - mean_ref[rows, :]) * inverse
        grad = swapped(normed_grad[rows, :])
        in_term[...] += jnp.sum((grad * centred).reshape(4, 8, D), 0)
        p = grad * gain[...]
        change = inverse * (
            p - jnp.mean(p, -1, keepdims=True) - centred * jnp.mean(p * centred, -1, keepdims=True)
        )
        result[rows, :] = (cotangent[rows, :].astype(F32) + change).astype(BF16)


def edges(net, place, padded):
    tm = lax.axis_index("tm")
    rows = {"first": padded.at[:, 16:32, :], "last": padded.at[:, FRAMES : FRAMES + 16, :]}
    before, after = padded.at[:, 0:16, :], padded.at[:, FRAMES + 16 : FRAMES + 32, :]
    here = (lax.axis_index("utt"), lax.axis_index("wshard"))
    ahead = (here[0], around(tm, 1), here[1])
    behind = (here[0], around(tm, 3), here[1])
    slots = (net.send(rows["last"], before, ahead), net.send(rows["first"], after, behind))

    def arrive():
        net.wait(slots[0], before)
        net.wait(slots[1], after)
        padded[:, 0:16, :] = padded[:, 0:16, :] * (tm > 0).astype(F32)
        padded[:, FRAMES + 16 : FRAMES + 32, :] = padded[:, FRAMES + 16 : FRAMES + 32, :] * (
            tm < 3
        ).astype(F32)

    return arrive


def module_kernel(scale, tree, *refs):
    (
        length_ref, frames_hbm, cotangent_hbm, norm_gain_hbm, in_hbm, taps, mid_gain_hbm, out_hbm,
        mixed_hbm, grad_frames_hbm, grad_in, grad_out, grad_taps, grad_norm_hbm, grad_mid_hbm,
    ) = refs[:15]
    (
        in_full, out_full, frames, branch_grad, normed, smooth, linear, opened, padded, grad_padded,
        temporal, smooth_grad, hidden_grad, normed_t, smooth_t, other_t, mean_ref, inverse_ref,
        sums, mid_term, in_term, first_terms, second_terms, small, small_sum, tiny, tiny_sum,
        norm_gain, mid_gain, grad_norm_gain, grad_mid_gain, sent, landed, local, bufs,
    ) = jax.tree_util.tree_unflatten(tree, refs[15:])
    place = Place()
    net = Net(place, sent, landed)
    c = place.c
    sibling = place.sibling()
    length = length_ref[0]
    start = lax.axis_index("tm") * FRAMES

    def valid(first, rows):
        return valid_rows(length, start, first, rows)

    loads = [
        pltpu.make_async_copy(in_hbm, in_full.at[c, place.y, place.z], local.at[0]),
        pltpu.make_async_copy(frames_hbm, frames, local.at[1]),
        pltpu.make_async_copy(cotangent_hbm, branch_grad.at[0:FRAMES], local.at[2]),
        pltpu.make_async_copy(out_hbm, out_full.at[c, place.y, place.z], local.at[3]),
        pltpu.make_async_copy(norm_gain_hbm, norm_gain.at[0], local.at[4]),
        pltpu.make_async_copy(mid_gain_hbm, mid_gain.at[0], local.at[5]),
    ]
    for load in loads:
        load.start()
    place.greet()
    gather_in, gather_out = Gather(net, place, in_full), Gather(net, place, out_full)
    loads[0].wait()
    gather_in.begin()
    loads[1].wait()
    loads[4].wait()
    loads[5].wait()
    norm = (frames, norm_gain, normed, mean_ref, inverse_ref)
    norm_stage(0, 6, *norm)
    gather_in.second()
    norm_stage(6, 16, *norm)
    out_first = net.count
    loads[3].wait()
    gather_out.begin()
    gather_in.third()
    loads[2].wait()

    @pl.loop(0, 8)
    def _(i):
        rows = rows_of(i, 64)
        branch_grad[rows, :] = (branch_grad[rows, :].astype(F32) * valid(i * 64, 64)).astype(BF16)

    pair_branch = net.send(branch_grad.at[0:FRAMES], branch_grad.at[FRAMES : 2 * FRAMES], sibling)
    transpose_stage(normed, normed_t.at[:, 0:FRAMES], other_t, c)
    pair_normed = net.send(other_t, normed_t.at[:, FRAMES : 2 * FRAMES], sibling)
    gather_out.second()
    gather_in.fourth()
    gather_in.finish()
    hidden = (normed, in_full, linear, opened, padded, valid)
    hidden_stage(0, 3, *hidden)
    gather_out.third()
    hidden_stage(3, 6, *hidden)
    arrive = edges(net, place, padded)
    gather_out.fourth()
    conv_stage((128, 256), padded, taps, temporal)
    arrive()
    conv_stage((0, 384), padded, taps, temporal)
    gather_out.finish()
    out_last = net.count
    for core in range(2):
        back_product(core, branch_grad.at[0:FRAMES], out_full, smooth_grad)
    mid_stage(temporal, mid_gain, smooth_grad, smooth, grad_padded, mid_term)
    arrive = edges(net, place, grad_padded)

    net.gone([pair_normed])
    transpose_stage(smooth, smooth_t.at[:, 0:FRAMES], other_t, c)
    pair_smooth = net.send(other_t, smooth_t.at[:, FRAMES : 2 * FRAMES], sibling)
    branch_stage(smooth, out_full, frames, valid, normed)
    store_mixed = pltpu.make_async_copy(normed, mixed_hbm, local.at[0])
    store_mixed.start()
    net.wait(pair_branch, branch_grad.at[FRAMES : 2 * FRAMES])
    net.wait(pair_smooth, smooth_t.at[:, FRAMES : 2 * FRAMES])
    weight_grad(smooth_t, branch_grad, lambda t: t * HALF, first_terms)
    scatter_out = Scatter(net, place, first_terms, bufs[0])
    scatter_out.step_far()
    arrive()
    conv = (padded, grad_padded, taps, linear, opened, valid, hidden_grad, sums)
    pair_hidden = []

    def backward(group):
        backward_conv(2 * group, 2 * group + 2, *conv)
        for column in (256 * group, D + 256 * group):
            own = hidden_grad.at[0:FRAMES, column : column + 256]
            there = hidden_grad.at[FRAMES : 2 * FRAMES, column : column + 256]
            pair_hidden.append((net.send(own, there, sibling), there))

    def hidden_arrive(groups):
        for _ in range(2 * groups):
            net.wait(*pair_hidden.pop(0))

    def grad_half(half, target):
        weight_grad(normed_t, hidden_grad, lambda t: t * D + half * HALF, target)

    third_terms = out_full.at[0]
    scatter_one = Scatter(net, place, second_terms, bufs[1])
    scatter_two = Scatter(net, place, third_terms, bufs[2])
    backward(0)
    backward(1)
    backward(2)
    scatter_out.step_near()
    net.wait(pair_normed, normed_t.at[:, FRAMES : 2 * FRAMES])
    hidden_arrive(3)
    grad_half(0, second_terms)
    scatter_one.step_far()
    backward(3)
    backward(4)
    backward(5)
    for i in range(12):
        lanes = slice((i % 2) * 128, (i % 2) * 128 + 128)
        columns = slice(i * 128, i * 128 + 128)
        core, portion = (i // 2) % 2, i // 4
        small[core, portion, 0:31, lanes] = jnp.sum(sums[i], 1)[0:31]
        small[core, portion, 31:32, lanes] = jnp.sum(mid_term[:, columns], 0, keepdims=True)
    total = Total(net, place, small, *bufs[3], small_sum)
    total.to_sibling()
    scatter_one.step_near()
    scatter_out.step_second()
    net.gone(range(out_first, out_last))
    hidden_arrive(3)
    grad_half(1, third_terms)
    scatter_two.step_far()
    total.begin()
    scatter_out.step_third()
    scatter_one.step_second()
    reload = pltpu.make_async_copy(cotangent_hbm, opened, local.at[1])
    reload.start()

    def store_out(column, value):
        grad_out[:, column : column + 128] = value * scale

    def store_in(half):
        def store(column, value):
            to = half * HALF + column + (HALF if column >= HALF else 0)
            grad_in[:, to : to + 128] = value * scale

        return store

    own_hidden = hidden_grad.at[0:FRAMES]
    back_product(0, own_hidden, in_full, temporal)
    total.step(1)
    scatter_two.step_near()
    back_product(1, own_hidden, in_full, temporal)
    scatter_one.step_third()
    scatter_out.step_spread()
    total.step(2)
    reload.wait()
    frames_stage(
        frames, opened, norm_gain, mean_ref, inverse_ref, temporal, smooth, in_term
    )
    store_frames = pltpu.make_async_copy(smooth, grad_frames_hbm, local.at[2])
    store_frames.start()
    for i in range(12):
        lanes = slice((i % 2) * 128, (i % 2) * 128 + 128)
        tiny[(i // 2) % 2, i // 4, :, lanes] = in_term[:, i * 128 : i * 128 + 128]
    rest = Total(net, place, tiny, *bufs[4], tiny_sum)
    rest.to_sibling()
    scatter_two.step_second()
    rest.begin()
    total.spread()
    scatter_one.step_spread()
    scatter_out.step_last(store_out)
    rest.step(1)
    scatter_two.step_third()
    scatter_one.step_last(store_in(0))
    rest.step(2)
    scatter_two.step_spread()
    total.last()
    rest.spread()
    for core in range(2):
        for portion in range(3):
            columns = slice(portion * 512 + core * 256, portion * 512 + core * 256 + 256)
            grad_taps[:, columns] = small_sum[core, portion, 0:31, :] * scale
            grad_mid_gain[:, columns] = small_sum[core, portion, 31:32, :] * scale
    scatter_two.step_last(store_in(1))
    rest.last()
    for core in range(2):
        for portion in range(3):
            columns = slice(portion * 512 + core * 256, portion * 512 + core * 256 + 256)
            grad_norm_gain[:, columns] = (
                jnp.sum(tiny_sum[core, portion], 0, keepdims=True) * scale
            )
    stores = [
        pltpu.make_async_copy(grad_norm_gain.at[0], grad_norm_hbm, local.at[4]),
        pltpu.make_async_copy(grad_mid_gain.at[0], grad_mid_hbm, local.at[5]),
    ]
    for store in stores:
        store.start()
    store_mixed.wait()
    store_frames.wait()
    for store in stores:
        store.wait()
    net.drain()


def settle_kernel(count, *refs):
    sources, targets, held = refs[:count], refs[count : 2 * count], refs[2 * count : -2]
    into, out = refs[-2:]
    first = [
        pltpu.make_async_copy(src, buf, into.at[i])
        for i, (src, buf) in enumerate(zip(sources, held))
    ]
    second = [
        pltpu.make_async_copy(buf, dst, out.at[i])
        for i, (buf, dst) in enumerate(zip(held, targets))
    ]
    for copy in first:
        copy.start()
    for arrived, copy in zip(first, second):
        arrived.wait()
        copy.start()
    for copy in second:
        copy.wait()


def settle(*arrays):
    arrays = [a[None] if i < 2 else a for i, a in enumerate(arrays)]
    count = len(arrays)
    outside = pl.BlockSpec(memory_space=pltpu.HBM)
    return tuple(
        pl.pallas_call(
            functools.partial(settle_kernel, count),
            out_shape=[jax.ShapeDtypeStruct(a.shape, a.dtype) for a in arrays],
            in_specs=[outside] * count,
            out_specs=[outside] * count,
            scratch_shapes=[pltpu.VMEM(a.shape, a.dtype) for a in arrays]
            + [pltpu.SemaphoreType.DMA((count,)), pltpu.SemaphoreType.DMA((count,))],
        )(*arrays)
    )


def body(frames, lengths, cotangent, norm_gain, w_in, kernel, mid_gain, w_out):
    scale = 1.0 / math.sqrt(
        FRAMES * lax.axis_size("utt") * lax.axis_size("tm") * lax.axis_size("wshard")
    )
    block = (FRAMES, D)
    copies = 2 * GATHER_COPIES + 3 * SCATTER_COPIES + 2 * TOTAL_COPIES + 32
    scratch = [
        pltpu.VMEM((2, 4, 4, ROWS, 2 * D), BF16),
        pltpu.VMEM((2, 4, 4, ROWS, D), BF16),
        pltpu.VMEM(block, BF16),
        pltpu.VMEM((2 * FRAMES, D), BF16),
        pltpu.VMEM(block, BF16),
        pltpu.VMEM(block, BF16),
        pltpu.VMEM(block, BF16),
        pltpu.VMEM(block, BF16),
        pltpu.VMEM((12, FRAMES + 32, 128), F32),
        pltpu.VMEM((12, FRAMES + 32, 128), F32),
        pltpu.VMEM(block, F32),
        pltpu.VMEM(block, BF16),
        pltpu.VMEM((2 * FRAMES, 2 * D), BF16),
        pltpu.VMEM((HALF, 2 * FRAMES), BF16),
        pltpu.VMEM((HALF, 2 * FRAMES), BF16),
        pltpu.VMEM((HALF, FRAMES), BF16),
        pltpu.VMEM((FRAMES, 1), F32),
        pltpu.VMEM((FRAMES, 1), F32),
        pltpu.VMEM((12, 32, 8, 128), F32),
        pltpu.VMEM((8, D), F32),
        pltpu.VMEM((8, D), F32),
        pltpu.VMEM((4, 4, ROWS, D), BF16),
        pltpu.VMEM((4, 4, ROWS, D), BF16),
        pltpu.VMEM((2, 3, 32, 256), F32),
        pltpu.VMEM((2, 3, 32, 256), F32),
        pltpu.VMEM((2, 3, 8, 256), F32),
        pltpu.VMEM((2, 3, 8, 256), F32),
        pltpu.VMEM((1, D), F32),
        pltpu.VMEM((1, D), F32),
        pltpu.VMEM((1, D), F32),
        pltpu.VMEM((1, D), F32),
        pltpu.SemaphoreType.DMA((copies,)),
        pltpu.SemaphoreType.DMA((copies,)),
        pltpu.SemaphoreType.DMA((6,)),
        [Scatter.scratch(D), Scatter.scratch(D), Scatter.scratch(D), Total.scratch(32, 256), Total.scratch(8, 256)],
    ]
    leaves, tree = jax.tree_util.tree_flatten(scratch)
    anywhere = pl.BlockSpec(memory_space=pl.ANY)
    inside = pl.BlockSpec(memory_space=pltpu.VMEM)
    scalar = pl.BlockSpec(memory_space=pltpu.SMEM)
    outs = pl.pallas_call(
        functools.partial(module_kernel, scale, tree),
        out_shape=[
            jax.ShapeDtypeStruct(block, BF16),
            jax.ShapeDtypeStruct(block, BF16),
            jax.ShapeDtypeStruct((ROWS, 2 * D), F32),
            jax.ShapeDtypeStruct((ROWS, D), F32),
            jax.ShapeDtypeStruct((31, D), F32),
            jax.ShapeDtypeStruct((D,), F32),
            jax.ShapeDtypeStruct((D,), F32),
        ],
        in_specs=[scalar, anywhere, anywhere, anywhere, anywhere, inside, anywhere, anywhere],
        out_specs=[anywhere, anywhere, inside, inside, inside, anywhere, anywhere],
        scratch_shapes=leaves,
        compiler_params=pltpu.CompilerParams(
            collective_id=0, has_side_effects=True, vmem_limit_bytes=63 * 2**20
        ),
    )(
        lengths, frames[0], cotangent[0], norm_gain, w_in, kernel, mid_gain, w_out
    )
    return settle(*outs)


def solution(mesh):
    return jax.shard_map(
        body,
        mesh=mesh,
        in_specs=(
            P(("utt", "wshard"), "tm", None),
            P(("utt", "wshard")),
            P(("utt", "wshard"), "tm", None),
            P(),
            P(("tm", "wshard"), None),
            P(),
            P(),
            P(("tm", "wshard"), None),
        ),
        out_specs=(
            P(("utt", "wshard"), "tm", None),
            P(("utt", "wshard"), "tm", None),
            P(("tm", "wshard"), None),
            P(("tm", "wshard"), None),
            P(),
            P(),
            P(),
        ),
        check_vma=False,
    )
```
